512 devices in a mesh: runs: 32 (over x, y), rank: 16 (over z, core).
Axes of the slice: x: 4, y: 8, z: 8, core: 2. Of those that a mesh axis runs over, the one named last changes fastest.
Arguments:
- inverse_cov: bfloat16 [163840, 5120], P(('runs', 'rank')), as said below
- panel_one: bfloat16 [163840, 256], P(('runs', 'rank')), as said below
- panel_two: bfloat16 [163840, 256], P(('runs', 'rank')), as said below
- response: float32 [163840], P(('runs', 'rank')), may hold values from -8 to 8
- inputs: float32 [6, 163840], P(None, ('runs', 'rank')), may hold values from -1 to 1
- coeffs: float32 [1024], replicated, may hold values from -0.1875 to 0.1875
- degrees: int32 [6, 1024], replicated, may hold values from 0 to 7, as said below
Outputs:
- alpha: float32 [163840], P(('runs', 'rank'))
The draws below stay inside these ranges and needn't reach their ends.
Inputs may be any that keep to these rules, and one draw needn't show every extreme that they name: Each leaf's block of inverse_cov is symmetric. `panel_one`: entries lie within 10 / sqrt(5120) of zero. `panel_two`: entries lie within 10 / sqrt(5120) of zero. `degrees`: the 1024 columns are distinct multi-indices, each of total degree at most 7.
All inputs are finite; a program needn't handle non-finite values.
Results may differ from the reference program's by a relative error of at most 0.0029.
Values may be sent and summed in bfloat16 or wider, within the bound.
A program may use at most 64 MiB of HBM per device.

```python
import math
import jax
import jax.numpy as jnp
import numpy as np
from jax import lax

R = 256
P_SIZE = 1024
DIMS = 6
LEAF = 5120
NROWS = 163840


def draw_inverse_cov(key, part):
    key = jax.random.fold_in(key, 7)
    leaves = NROWS // LEAF
    spread = 2.0 / LEAF ** 0.5

    def one_leaf(leaf_index):
        leaf_key = jax.random.fold_in(key, leaf_index)
        key_off, key_diag = jax.random.split(leaf_key)
        entries = jax.random.uniform(key_off, (LEAF, LEAF), jnp.float32, -1.0, 1.0) * spread
        diagonal = jax.random.uniform(key_diag, (LEAF,), jnp.float32, 3.0, 6.0)
        upper = jnp.triu(entries, 1)
        return (upper + upper.T + jnp.diag(diagonal)).astype(jnp.bfloat16)
    return lax.map(one_leaf, jnp.arange(leaves)).reshape(leaves * LEAF, LEAF)


def factor_panel(key, noise, decay):
    quads = NROWS // (4 * LEAF)
    width = noise.shape[1]
    key_rows, key_cols = jax.random.split(key)
    row_loads = jax.random.normal(key_rows, (16, quads, 4 * LEAF), jnp.float32)
    col_loads = jax.random.normal(key_cols, (16, quads, width), jnp.float32)
    total = noise.reshape(quads, 4 * LEAF, width)
    strength = 1.0
    for factor_index in range(16):
        total = total + strength * row_loads[factor_index][:, :, None] * col_loads[factor_index][:, None, :]
        strength = strength * decay
    unit = LEAF ** (-0.5)
    return jnp.clip(total * unit, -10.0 * unit, 10.0 * unit).reshape(NROWS, width).astype(jnp.bfloat16)


def draw_panel_one(key, part):
    key = jax.random.fold_in(key, 13)
    key_noise, key_factor = jax.random.split(key)
    noise = jax.random.normal(key_noise, (NROWS, R), jnp.float32)
    return factor_panel(key_factor, noise, 0.75)


def draw_panel_two(key, part):
    key = jax.random.fold_in(key, 17)
    key_noise, key_factor = jax.random.split(key)
    noise = jax.random.normal(key_noise, (NROWS, R), jnp.float32)
    return factor_panel(key_factor, noise, 0.75)


def index_table():
    others = []
    for first in range(8):
        for second in range(8):
            for third in range(8):
                for fourth in range(8):
                    for fifth in range(8):
                        for sixth in range(8):
                            entry = (first, second, third, fourth, fifth, sixth)
                            if sum(entry) <= 7 and entry != (7, 0, 0, 0, 0, 0):
                                others.append(entry)
    return np.array([(7, 0, 0, 0, 0, 0)] + others, dtype=np.int32)


def draw_degrees(key, part):
    key = jax.random.fold_in(key, 11)
    table = jnp.asarray(index_table())
    count = table.shape[0]
    picked = jax.random.permutation(key, count - 1)[:P_SIZE - 1] + 1
    chosen = jnp.concatenate([jnp.zeros((1,), jnp.int32), picked.astype(jnp.int32)])
    return table[chosen].T.astype(jnp.int32)


def block_levels(key, shape, pieces, least, high):
    level = 1.0
    for axis_at, blocks in pieces:
        draws = jax.random.uniform(jax.random.fold_in(jax.random.fold_in(key, 6), axis_at), (blocks,), jnp.float32, least / len(pieces), high / len(pieces))
        level = level * jnp.repeat(jnp.exp(draws), shape[axis_at] // blocks).reshape((-1,) + (1,) * (len(shape) - 1 - axis_at))
    return level


def normal_values(rng, shape, deviation, limit, shards=(), held_as=jnp.bfloat16):
    values = deviation * jax.random.normal(rng, shape, jnp.float32)
    if shards:
        values = values * block_levels(rng, shape, shards, -0.22, 0.18)
    return jnp.clip(values, -limit, limit).astype(held_as)


def setup_inputs(seed: int = 0) -> dict:
    key_list = jax.random.split(jax.random.key(seed), 8)
    inverse_cov = draw_inverse_cov(jax.random.fold_in(key_list[7], 71), 0)
    panel_one = draw_panel_one(jax.random.fold_in(key_list[7], 71), 0)
    panel_two = draw_panel_two(jax.random.fold_in(key_list[7], 71), 0)
    response = normal_values(key_list[3], (NROWS,), 1.5, 8.0, ((0, 512),), jnp.float32)
    inputs = jnp.clip(jax.random.uniform(key_list[4], (DIMS, NROWS), jnp.float32, -1.0, 1.0) * block_levels(key_list[4], (DIMS, NROWS), ((1, 512),), -0.4, 0.0), -1.0, 1.0)
    coeffs = normal_values(key_list[5], (P_SIZE,), P_SIZE ** -0.5, 0.1875, (), jnp.float32)
    degrees = draw_degrees(jax.random.fold_in(key_list[7], 71), 0)
    return dict(inverse_cov=inverse_cov, panel_one=panel_one, panel_two=panel_two, response=response, inputs=inputs, coeffs=coeffs, degrees=degrees)


ROOT_THREE = 1.7320508075688772

def legendre_basis(inputs, degrees):
    basis_rows = None
    for column in range(inputs.shape[0]):
        points = inputs[column][:, None]
        orders = degrees[column][None, :]
        previous = jnp.ones_like(points)
        current = points
        factor = jnp.where(orders == 0, jnp.float32(1.0), ROOT_THREE * points)
        for level in range(1, 7):
            following = ((2 * level + 1) * points * current - level * previous) / (level + 1)
            factor = jnp.where(orders == level + 1, math.sqrt(2 * level + 3) * following, factor)
            previous, current = (current, following)
        basis_rows = factor if basis_rows is None else basis_rows * factor
    return basis_rows

def project_rows(panel, field):
    return jnp.dot(panel.astype(jnp.float32).T, field, precision=lax.Precision.HIGHEST)

def factorize(gram):
    extent = gram.shape[0]
    shifted = 0.5 * (gram + gram.T) + jnp.eye(extent, dtype=jnp.float32)
    return jnp.linalg.cholesky(shifted)

def solve_with(factor, rhs):
    return jax.scipy.linalg.cho_solve((factor, True), rhs)

def highest(left, right):
    return jnp.dot(left, right, precision=lax.Precision.HIGHEST)

def one_quad(items):
    blocks, first, second, answers, points, coeffs, degrees = items
    solved = []
    for leaf in range(4):
        trend = highest(legendre_basis(points[:, leaf], degrees), coeffs)
        residual_b = (answers[leaf] - trend).astype(jnp.bfloat16)
        solved.append((jnp.dot(blocks[leaf].astype(jnp.float32), first[leaf].astype(jnp.float32), preferred_element_type=jnp.float32), jnp.dot(blocks[leaf].astype(jnp.float32), second[leaf].astype(jnp.float32), preferred_element_type=jnp.float32), jnp.dot(blocks[leaf].astype(jnp.float32), residual_b.astype(jnp.float32), preferred_element_type=jnp.float32)))
    coupled_all = []
    weights_all = []
    for pair in range(2):
        left_leaf, right_leaf = (2 * pair, 2 * pair + 1)
        pair_gram = project_rows(first[left_leaf], solved[left_leaf][0]) + project_rows(first[right_leaf], solved[right_leaf][0])
        pair_cross = project_rows(first[left_leaf], solved[left_leaf][1]) + project_rows(first[right_leaf], solved[right_leaf][1])
        pair_rhs = project_rows(first[left_leaf], solved[left_leaf][2]) + project_rows(first[right_leaf], solved[right_leaf][2])
        factor = factorize(pair_gram)
        mixing = solve_with(factor, pair_cross)
        shift = solve_with(factor, pair_rhs)
        for leaf in (left_leaf, right_leaf):
            coupled_all.append(solved[leaf][1] - highest(solved[leaf][0], mixing))
            weights_all.append(solved[leaf][2] - highest(solved[leaf][0], shift))
    quad_gram = jnp.zeros((first.shape[2], first.shape[2]), jnp.float32)
    quad_rhs = jnp.zeros((first.shape[2],), jnp.float32)
    for leaf in range(4):
        quad_gram = quad_gram + project_rows(second[leaf], coupled_all[leaf])
        quad_rhs = quad_rhs + project_rows(second[leaf], weights_all[leaf])
    gain = solve_with(factorize(quad_gram), quad_rhs)
    return jnp.stack([weights_all[leaf] - highest(coupled_all[leaf], gain) for leaf in range(4)])

def reference(inverse_cov, panel_one, panel_two, response, inputs, coeffs, degrees):
    quads = NROWS // (4 * LEAF)
    blocks = inverse_cov.reshape(quads, 4, LEAF, LEAF)
    first = panel_one.reshape(quads, 4, LEAF, R)
    second = panel_two.reshape(quads, 4, LEAF, R)
    answers = response.reshape(quads, 4, LEAF)
    points = jnp.moveaxis(inputs.reshape(DIMS, quads, 4, LEAF), 1, 0)

    def step_quad(items):
        return one_quad((items[0], items[1], items[2], items[3], items[4], coeffs, degrees))
    alpha = lax.map(step_quad, (blocks, first, second, answers, points))
    return alpha.reshape(NROWS)
```

```python
import math

import jax
import jax.numpy as jnp
import numpy as np
from jax import lax
from jax.experimental import pallas as pl
from jax.experimental.pallas import tpu as pltpu
from jax.sharding import PartitionSpec as P

MESH = pl.DeviceIdType.MESH
F32 = jnp.float32
BF16 = jnp.bfloat16
HIGHEST = lax.Precision.HIGHEST
RANK = 256
HALF = 128
CHIPS = 8
WIDE = 768
PART = 640


def degree_tables():
    triples = [
        (a, b, c) for a in range(8) for b in range(8) for c in range(8) if a + b + c <= 7
    ]
    codes = np.full((HALF, 1), -1, np.int32)
    picks = np.zeros((6, HALF, 64), np.float32)
    for row, triple in enumerate(triples):
        codes[row, 0] = triple[0] + 8 * triple[1] + 64 * triple[2]
        for column in range(6):
            picks[column, row, triple[column % 3] * 8 + column] = 1.0
    return codes, picks.reshape(6 * HALF, 64)


def dot(left, right, dims=((1,), (0,)), precision=None):
    return lax.dot_general(
        left, right, (dims, ((), ())), precision=precision, preferred_element_type=F32
    )


def high(left, right, dims=((1,), (0,))):
    return dot(left, right, dims, HIGHEST)


def split(value):
    upper = value.astype(BF16)
    return upper, (value - upper.astype(F32)).astype(BF16)


def gather_kernel(
    cov_ref, one_ref, two_ref, response_ref, inputs_ref, coeffs_ref, degrees_ref, codes_ref,
    picks_ref, grams_ref, solved_ref, residue_ref,
    cov, panels, points, own_res, all_res, parts, from_core, mine, from_chips, leaf_sum,
    from_leaves, local_sem, panel_send, panel_recv, core_send, core_recv, res_send, res_recv,
    pick_send, pick_recv, sum_send, sum_recv, chip_send, chip_recv, leaf_send, leaf_recv,
    gram_send, gram_recv, pair_send, pair_recv,
):
    leaf = lax.axis_index("runs")
    place = lax.axis_index("rank")
    chip, core = place // 2, place % 2
    rows = one_ref.shape[0]
    own_rows = pl.ds(pl.multiple_of(core * rows, 64), rows)

    def on(offset):
        return lax.rem(chip + offset + CHIPS, CHIPS)

    def chip_at(offset):
        return (leaf, 2 * on(offset) + core)

    sibling = (leaf, 2 * chip + 1 - core)

    def leaf_at(bits):
        return (leaf ^ bits, place)

    peers = [chip_at(o) for o in range(1, CHIPS)] + [sibling] + [leaf_at(b) for b in (1, 2, 3)]
    barrier = pltpu.get_barrier_semaphore()
    for peer in peers:
        pl.semaphore_signal(barrier, inc=1, device_id=peer, device_id_type=MESH)

    operands = (one_ref, two_ref)
    local = [
        pltpu.make_async_copy(one_ref, panels.at[0, chip, own_rows], local_sem.at[0]),
        pltpu.make_async_copy(two_ref, panels.at[1, chip, own_rows], local_sem.at[1]),
        pltpu.make_async_copy(cov_ref, cov, local_sem.at[2]),
    ]
    for copy in local:
        copy.start()
    pl.semaphore_wait(barrier, len(peers))

    sent = []

    def push(src, dst, send, recv, device):
        copy = pltpu.make_async_remote_copy(
            src_ref=src, dst_ref=dst, send_sem=send, recv_sem=recv, device_id=device,
            device_id_type=MESH,
        )
        copy.start()
        sent.append(copy)
        return copy

    class Ring:
        def __init__(self, view, own, steps, send, recv, core_sends, core_recvs):
            self.view, self.own, self.steps = view, own, steps
            self.send, self.recv = send, recv
            self.core_sends, self.core_recvs = core_sends, core_recvs
            self.flying, self.handed = {}, {}

        def forward(self, way, step, src):
            offset = -(step - 1) if way == 0 else step - 1
            self.flying[way, step] = push(
                src, self.view(on(offset), core), self.send.at[way, step - 1],
                self.recv.at[way, step - 1], chip_at(1 if way == 0 else -1),
            )

        def hand(self, way, step, src):
            offset = -step if way == 0 else step
            slot = 4 * way + step
            self.handed[way, step] = push(
                src, self.view(on(offset), core), self.core_sends.at[slot],
                self.core_recvs.at[slot], sibling,
            )

        def start(self):
            for way in (0, 1):
                self.forward(way, 1, self.own)
            if self.core_sends is not None:
                self.hand(0, 0, self.own)

        def arrive(self, way, step):
            if step > self.steps[way]:
                return
            self.flying[way, step].wait_recv()
            block = self.view(on(-step if way == 0 else step), core)
            if step < self.steps[way]:
                self.forward(way, step + 1, block)
            if self.core_sends is not None:
                self.hand(way, step, block)

        def handed_over(self, way, step):
            if (way, step) in self.handed:
                self.handed[way, step].wait_recv()

    rings = [
        Ring(
            lambda zz, cc, k=k: panels.at[k, zz, pl.ds(pl.multiple_of(cc * rows, 64), rows)],
            operands[k], (4 - k, 3 + k), panel_send.at[k], panel_recv.at[k], core_send.at[k],
            core_recv.at[k],
        )
        for k in (0, 1)
    ]
    for ring in rings:
        ring.start()

    points[...] = jnp.zeros(points.shape, F32)
    points[0:6, :] = inputs_ref[...]
    x = points[...]
    levels = [jnp.ones_like(x), x]
    for k in range(1, 7):
        levels.append(((2 * k + 1) * x * levels[k] - k * levels[k - 1]) / (k + 1))
    levels = [math.sqrt(2 * k + 1) * level for k, level in enumerate(levels)]
    factors = high(picks_ref[...], jnp.concatenate(levels, axis=0))
    first = factors[0:128] * factors[128:256] * factors[256:384]
    second = factors[384:512] * factors[512:640] * factors[640:768]
    orders = degrees_ref[...]
    left_code = orders[0:1] + 8 * orders[1:2] + 64 * orders[2:3]
    right_code = orders[3:4] + 8 * orders[4:5] + 64 * orders[5:6]
    left = jnp.where(codes_ref[...] == left_code, coeffs_ref[...], 0.0)
    right = jnp.where(codes_ref[...] == right_code, jnp.float32(1.0), 0.0)
    table = high(left, right, ((1,), (1,)))
    trend = jnp.sum(high(table, first, ((0,), (0,))) * second, axis=0, keepdims=True)
    residual = (response_ref[...] - trend).astype(BF16).astype(F32)
    residual8 = jnp.broadcast_to(residual, (8, rows))
    own_res[0] = jnp.zeros((8, 2 * rows), F32)

    @pl.when(core == 0)
    def _():
        own_res[0, :, 0:rows] = residual8

    @pl.when(core == 1)
    def _():
        own_res[0, :, rows : 2 * rows] = residual8

    res_copy = push(own_res.at[0], own_res.at[1], pick_send, pick_recv, sibling)
    for copy in local:
        copy.wait()

    def apply(offset, fresh=False):
        at = on(offset)
        block = cov[:, pl.ds(pl.multiple_of(at * 2 * rows, 128), 2 * rows)]
        for k in (0, 1):
            term = dot(block, panels[k, at])
            lanes = slice(RANK * k, RANK * (k + 1))
            solved_ref[:, lanes] = term if fresh else solved_ref[:, lanes] + term

    res_ring = Ring(
        lambda zz, cc: all_res.at[zz], all_res.at[chip], (4, 3), res_send, res_recv, None, None
    )
    for step in range(1, 5):
        for ring in rings:
            ring.arrive(0, step)
            ring.arrive(1, step)
        if step == 1:
            res_copy.wait_recv()
            all_res[chip] = own_res[0] + own_res[1]
            res_ring.start()
        else:
            res_ring.arrive(0, step - 1)
            res_ring.arrive(1, step - 1)
        for ring in rings:
            ring.handed_over(0, step - 1)
            ring.handed_over(1, step - 1)
        apply(step - 1 if step > 1 else 0, step == 1)
        if step > 1:
            apply(1 - step)
    res_ring.arrive(0, 4)
    for ring in rings:
        ring.handed_over(0, 4)
        ring.handed_over(1, 4)
    apply(4)

    one_t = panels[0, chip, own_rows]
    two_t = panels[1, chip, own_rows]
    upper, lower = split(solved_ref[...])
    inner = ((0,), (0,))
    gram = dot(one_t, upper, inner) + dot(one_t, lower, inner)
    parts[0, :, 0:512] = gram[0:128]
    parts[1, :, 0:384] = gram[128:256, 128:512]
    gram = dot(two_t, upper[:, 256:512], inner) + dot(two_t, lower[:, 256:512], inner)
    parts[0, :, 512:640] = gram[0:128, 128:256]
    parts[0, :, 640:768] = jnp.zeros((HALF, HALF), F32)
    parts[1, :, 512:640] = gram[0:128, 0:128]
    parts[1, :, 640:768] = gram[128:256, 128:256]
    residual_b = residual8.astype(BF16)
    rhs = dot(residual_b, upper) + dot(residual_b, lower)
    line = lax.broadcasted_iota(jnp.int32, (8, HALF), 0)
    packed = jnp.zeros((8, HALF), F32)
    for k in range(4):
        packed = jnp.where(line == k, rhs[:, HALF * k : HALF * (k + 1)], packed)
    parts[1, :, 384:512] = jnp.zeros((HALF, HALF), F32)
    parts[1, 0:8, 384:512] = packed

    swap = push(parts.at[1 - core], from_core, sum_send, sum_recv, sibling)

    def residue(zz, total):
        lanes = pl.ds(pl.multiple_of(zz * 2 * rows, 128), 2 * rows)
        return total + dot(all_res[zz].astype(BF16), cov[:, lanes], ((1,), (1,)))

    residue_ref[...] = lax.fori_loop(0, CHIPS, residue, jnp.zeros((8, rows), F32))
    swap.wait_recv()
    for k in range(CHIPS):
        band = slice(16 * k, 16 * (k + 1))
        mine[k] = parts[core, band] + from_core[band]

    copies = [
        push(
            mine.at[on(o)], from_chips.at[o - 1], chip_send.at[o - 1], chip_recv.at[o - 1],
            chip_at(o),
        )
        for o in range(1, CHIPS)
    ]
    total = mine[chip]
    for o in range(1, CHIPS):
        copies[o - 1].wait_recv()
        total = total + from_chips[o - 1]
    leaf_sum[...] = total

    copies = [
        push(leaf_sum, from_leaves.at[b - 1], leaf_send.at[b - 1], leaf_recv.at[b - 1], leaf_at(b))
        for b in (1, 2, 3)
    ]
    copies[0].wait_recv()
    near = total + from_leaves[0]
    copies[1].wait_recv()
    copies[2].wait_recv()
    far = from_leaves[1] + from_leaves[2]
    grams_ref[0, chip, core, :, 0:512] = near[:, 0:512]
    grams_ref[1, chip, core, :, 0:512] = far[:, 0:512]
    grams_ref[0, chip, core, :, 512:640] = near[:, 512:640] + far[:, 512:640]
    grams_ref[1, chip, core, :, 512:640] = near[:, 640:768] + far[:, 640:768]

    rings = [
        Ring(
            lambda zz, cc, k=k: grams_ref.at[k, zz, cc], grams_ref.at[k, chip, core],
            (4 - k, 3 + k), gram_send.at[k], gram_recv.at[k], pair_send.at[k], pair_recv.at[k],
        )
        for k in (0, 1)
    ]
    for ring in rings:
        ring.start()
    for step in range(1, 5):
        for ring in rings:
            ring.arrive(0, step)
            ring.arrive(1, step)
    for ring in rings:
        for step in range(0, 5):
            ring.handed_over(0, step)
            ring.handed_over(1, step)
    for copy in sent:
        copy.wait_send()


def invert(matrices):
    lane = lax.broadcasted_iota(jnp.int32, (1, HALF), 1)
    line = lax.broadcasted_iota(jnp.int32, (HALF, 1), 0)
    wide = (1, HALF)
    for k in range(0, HALF, 2):
        pivot = (lane == k) | (lane == k + 1)
        swept = []
        for a in matrices:
            r0, r1 = a[k : k + 1], a[k + 1 : k + 2]
            c0, c1 = a[:, k : k + 1], a[:, k + 1 : k + 2]
            p = jnp.broadcast_to(r0[:, k : k + 1], wide)
            q = jnp.broadcast_to(r0[:, k + 1 : k + 2], wide)
            s = jnp.broadcast_to(r1[:, k + 1 : k + 2], wide)
            scale = 1.0 / (p * s - q * q)
            i00, i01, i11 = s * scale, -q * scale, p * scale
            u0 = i00 * r0 + i01 * r1
            u1 = i01 * r0 + i11 * r1
            u0 = jnp.where(lane == k, -i00, jnp.where(lane == k + 1, -i01, u0))
            u1 = jnp.where(lane == k, -i01, jnp.where(lane == k + 1, -i11, u1))
            a = jnp.where(pivot, 0.0, a) - c0 * u0 - c1 * u1
            swept.append(jnp.where(line == k, u0, jnp.where(line == k + 1, u1, a)))
        matrices = swept
    return [-a for a in matrices]


def symmetric(block):
    return 0.5 * (block + block.T)


def solve_kernel(grams_ref, solved_ref, residue_ref, alpha_ref):
    line = lax.broadcasted_iota(jnp.int32, (HALF, HALF), 0)
    lane = lax.broadcasted_iota(jnp.int32, (HALF, HALF), 1)
    eye = jnp.where(line == lane, jnp.float32(1.0), 0.0)
    inner, outer = ((0,), (0,)), ((1,), (1,))

    def block(k, core, start, stop):
        return grams_ref[k, :, core, :, start:stop].reshape(HALF, stop - start)

    cross = [block(k, 0, 128, 256) for k in (0, 1)]
    top = [block(k, 0, 256, 512) for k in (0, 1)]
    bottom = [block(k, 1, 128, 384) for k in (0, 1)]
    rhs = [grams_ref[k, 0, 1, 0:8, 384:512] for k in (0, 1)]

    head = invert([eye + symmetric(block(k, 0, 0, 128)) for k in (0, 1)])
    tie = [high(head[k], cross[k]) for k in (0, 1)]
    tail = invert(
        [
            eye + symmetric(block(k, 1, 0, 128)) - symmetric(high(cross[k], tie[k], inner))
            for k in (0, 1)
        ]
    )
    second = [grams_ref[0, 0, 1, 0:8, 384:512] + grams_ref[1, 0, 1, 0:8, 384:512]][0]
    g_a, g_b, g_c = block(0, 1, 512, 640), block(0, 0, 512, 640), block(1, 1, 512, 640)
    q0 = jnp.broadcast_to(second[2:3], (8, HALF))
    q1 = jnp.broadcast_to(second[3:4], (8, HALF))
    rest = jnp.concatenate([q0, q1], axis=1)
    near = None
    for k in (0, 1):
        lower = bottom[k] - high(tie[k], top[k], inner)
        head_top = high(head[k], top[k])
        tail_low = high(tail[k], lower)
        g_a = g_a - high(top[k][:, 0:128], head_top[:, 0:128], inner)
        g_a = g_a - high(lower[:, 0:128], tail_low[:, 0:128], inner)
        g_b = g_b - high(top[k][:, 0:128], head_top[:, 128:256], inner)
        g_b = g_b - high(lower[:, 0:128], tail_low[:, 128:256], inner)
        g_c = g_c - high(top[k][:, 128:256], head_top[:, 128:256], inner)
        g_c = g_c - high(lower[:, 128:256], tail_low[:, 128:256], inner)
        f0 = jnp.broadcast_to(rhs[k][0:1], (8, HALF))
        f1 = jnp.broadcast_to(rhs[k][1:2], (8, HALF))
        f1_low = f1 - high(f0, tie[k])
        rest = rest - high(f0, head_top) - high(f1_low, tail_low)
        if k == 0:
            near = (f0, f1)

    def solve(first, mid, last, v0, v1):
        y1 = high(v1 - high(v0, mid), last)
        y0 = high(v0, first) - high(y1, mid, outer)
        return jnp.concatenate([y0, y1], axis=1)

    (quad_head,) = invert([eye + symmetric(g_a)])
    quad_tie = high(quad_head, g_b)
    (quad_tail,) = invert([eye + symmetric(g_c) - symmetric(high(g_b, quad_tie, inner))])
    gain = solve(quad_head, quad_tie, quad_tail, rest[:, 0:128], rest[:, 128:256])
    v0 = near[0] - high(gain, top[0], outer)
    v1 = near[1] - high(gain, bottom[0], outer)
    shift = solve(head[0], tie[0], tail[0], v0, v1)
    both = jnp.concatenate([shift, gain], axis=1)
    alpha = residue_ref[...] - high(both, solved_ref[...], outer)
    alpha_ref[...] = alpha[0:1]


def per_device(inverse_cov, panel_one, panel_two, response, inputs, coeffs, degrees):
    codes, picks = degree_tables()
    rows = panel_one.shape[0]
    vmem = pl.BlockSpec(memory_space=pltpu.VMEM)
    anywhere = pl.BlockSpec(memory_space=pl.ANY)
    dma = pltpu.SemaphoreType.DMA
    grams, solved, residue = pl.pallas_call(
        gather_kernel,
        out_shape=(
            jax.ShapeDtypeStruct((2, CHIPS, 2, 16, PART), F32),
            jax.ShapeDtypeStruct((rows, 2 * RANK), F32),
            jax.ShapeDtypeStruct((8, rows), F32),
        ),
        in_specs=[anywhere] * 3 + [vmem] * 6,
        out_specs=(vmem, vmem, vmem),
        scratch_shapes=[
            pltpu.VMEM(inverse_cov.shape, BF16),
            pltpu.VMEM((2, CHIPS, 2 * rows, RANK), BF16),
            pltpu.VMEM((8, rows), F32),
            pltpu.VMEM((2, 8, 2 * rows), F32),
            pltpu.VMEM((CHIPS, 8, 2 * rows), F32),
            pltpu.VMEM((2, HALF, WIDE), F32),
            pltpu.VMEM((HALF, WIDE), F32),
            pltpu.VMEM((CHIPS, 16, WIDE), F32),
            pltpu.VMEM((CHIPS - 1, 16, WIDE), F32),
            pltpu.VMEM((16, WIDE), F32),
            pltpu.VMEM((3, 16, WIDE), F32),
            dma((3,)),
            dma((2, 2, 4)), dma((2, 2, 4)),
            dma((2, 9)), dma((2, 9)),
            dma((2, 4)), dma((2, 4)),
            dma, dma,
            dma, dma,
            dma((CHIPS - 1,)), dma((CHIPS - 1,)),
            dma((3,)), dma((3,)),
            dma((2, 2, 4)), dma((2, 2, 4)),
            dma((2, 9)), dma((2, 9)),
        ],
        compiler_params=pltpu.CompilerParams(
            collective_id=0, has_side_effects=True, vmem_limit_bytes=40 * 1024 * 1024
        ),
    )(
        inverse_cov, panel_one, panel_two, response.reshape(1, rows), inputs,
        coeffs.reshape(1, -1), degrees, jnp.asarray(codes), jnp.asarray(picks),
    )
    alpha = pl.pallas_call(
        solve_kernel,
        out_shape=jax.ShapeDtypeStruct((1, rows), F32),
        in_specs=[vmem] * 3,
        out_specs=vmem,
        compiler_params=pltpu.CompilerParams(vmem_limit_bytes=40 * 1024 * 1024),
    )(grams, solved, residue)
    return alpha.reshape(rows)


def solution(mesh):
    in_specs = (
        P(("runs", "rank"), None),
        P(("runs", "rank"), None),
        P(("runs", "rank"), None),
        P(("runs", "rank")),
        P(None, ("runs", "rank")),
        P(),
        P(),
    )
    out_specs = P(("runs", "rank"))
    return jax.shard_map(
        per_device, mesh=mesh, in_specs=in_specs, out_specs=out_specs, check_vma=False
    )
```

```python
import math

import jax
import jax.numpy as jnp
import numpy as np
from jax import lax
from jax.experimental import pallas as pl
from jax.experimental.pallas import tpu as pltpu
from jax.sharding import PartitionSpec as P

MESH = pl.DeviceIdType.MESH
F32 = jnp.float32
BF16 = jnp.bfloat16
HIGHEST = lax.Precision.HIGHEST
RANK = 256
HALF = 128
CHIPS = 8
WIDE = 768
PART = 640


def degree_tables():
    triples = [
        (a, b, c) for a in range(8) for b in range(8) for c in range(8) if a + b + c <= 7
    ]
    codes = np.full((HALF, 1), -1, np.int32)
    picks = np.zeros((6, HALF, 64), np.float32)
    for row, triple in enumerate(triples):
        codes[row, 0] = triple[0] + 8 * triple[1] + 64 * triple[2]
        for column in range(6):
            picks[column, row, triple[column % 3] * 8 + column] = 1.0
    return codes, picks.reshape(6 * HALF, 64)


def dot(left, right, dims=((1,), (0,)), precision=None):
    return lax.dot_general(
        left, right, (dims, ((), ())), precision=precision, preferred_element_type=F32
    )


def high(left, right, dims=((1,), (0,))):
    return dot(left, right, dims, HIGHEST)


def split(value):
    upper = value.astype(BF16)
    return upper, (value - upper.astype(F32)).astype(BF16)


def gather_kernel(
    cov_ref, one_ref, two_ref, response_hbm, inputs_hbm, coeffs_hbm, degrees_hbm, codes_hbm,
    picks_hbm, grams_ref, solved_ref, residue_ref,
    response_ref, inputs_ref, coeffs_ref, degrees_ref, codes_ref, picks_ref, cov, panels, points, own_res, all_res, parts, from_core, mine, from_chips, leaf_sum,
    from_leaves, local_sem, panel_send, panel_recv, core_send, core_recv, res_send, res_recv,
    pick_send, pick_recv, sum_send, sum_recv, chip_send, chip_recv, leaf_send, leaf_recv,
    gram_send, gram_recv, pair_send, pair_recv,
):
    leaf = lax.axis_index("runs")
    place = lax.axis_index("rank")
    chip, core = place // 2, place % 2
    rows = one_ref.shape[0]
    own_rows = pl.ds(pl.multiple_of(core * rows, 64), rows)

    def on(offset):
        return lax.rem(chip + offset + CHIPS, CHIPS)

    def chip_at(offset):
        return (leaf, 2 * on(offset) + core)

    sibling = (leaf, 2 * chip + 1 - core)

    def leaf_at(bits):
        return (leaf ^ bits, place)

    peers = [chip_at(o) for o in range(1, CHIPS)] + [sibling] + [leaf_at(b) for b in (1, 2, 3)]
    barrier = pltpu.get_barrier_semaphore()
    for peer in peers:
        pl.semaphore_signal(barrier, inc=1, device_id=peer, device_id_type=MESH)

    operands = (one_ref, two_ref)
    local = [
        pltpu.make_async_copy(one_ref, panels.at[0, chip, own_rows], local_sem.at[0]),
        pltpu.make_async_copy(two_ref, panels.at[1, chip, own_rows], local_sem.at[1]),
        pltpu.make_async_copy(cov_ref, cov, local_sem.at[2]),
    ]
    small = [
        pltpu.make_async_copy(src, dst, local_sem.at[3 + k])
        for k, (src, dst) in enumerate(
            [
                (response_hbm, response_ref), (inputs_hbm, inputs_ref), (coeffs_hbm, coeffs_ref),
                (degrees_hbm, degrees_ref), (codes_hbm, codes_ref), (picks_hbm, picks_ref),
            ]
        )
    ]
    for copy in small:
        copy.start()
    for copy in local:
        copy.start()
    pl.semaphore_wait(barrier, len(peers))

    sent = []

    def push(src, dst, send, recv, device):
        copy = pltpu.make_async_remote_copy(
            src_ref=src, dst_ref=dst, send_sem=send, recv_sem=recv, device_id=device,
            device_id_type=MESH,
        )
        copy.start()
        sent.append(copy)
        return copy

    class Ring:
        def __init__(self, view, own, steps, send, recv, core_sends, core_recvs):
            self.view, self.own, self.steps = view, own, steps
            self.send, self.recv = send, recv
            self.core_sends, self.core_recvs = core_sends, core_recvs
            self.flying, self.handed = {}, {}

        def forward(self, way, step, src):
            offset = -(step - 1) if way == 0 else step - 1
            self.flying[way, step] = push(
                src, self.view(on(offset), core), self.send.at[way, step - 1],
                self.recv.at[way, step - 1], chip_at(1 if way == 0 else -1),
            )

        def hand(self, way, step, src):
            offset = -step if way == 0 else step
            slot = 4 * way + step
            self.handed[way, step] = push(
                src, self.view(on(offset), core), self.core_sends.at[slot],
                self.core_recvs.at[slot], sibling,
            )

        def start(self):
            for way in (0, 1):
                self.forward(way, 1, self.own)
            if self.core_sends is not None:
                self.hand(0, 0, self.own)

        def arrive(self, way, step):
            if step > self.steps[way]:
                return
            self.flying[way, step].wait_recv()
            block = self.view(on(-step if way == 0 else step), core)
            if step < self.steps[way]:
                self.forward(way, step + 1, block)
            if self.core_sends is not None:
                self.hand(way, step, block)

        def handed_over(self, way, step):
            if (way, step) in self.handed:
                self.handed[way, step].wait_recv()

    rings = [
        Ring(
            lambda zz, cc, k=k: panels.at[k, zz, pl.ds(pl.multiple_of(cc * rows, 64), rows)],
            operands[k], (4 - k, 3 + k), panel_send.at[k], panel_recv.at[k], core_send.at[k],
            core_recv.at[k],
        )
        for k in (0, 1)
    ]
    for ring in rings:
        ring.start()

    for copy in small:
        copy.wait()
    points[...] = jnp.zeros(points.shape, F32)
    points[0:6, :] = inputs_ref[...]
    x = points[...]
    levels = [jnp.ones_like(x), x]
    for k in range(1, 7):
        levels.append(((2 * k + 1) * x * levels[k] - k * levels[k - 1]) / (k + 1))
    levels = [math.sqrt(2 * k + 1) * level for k, level in enumerate(levels)]
    factors = high(picks_ref[...], jnp.concatenate(levels, axis=0))
    first = factors[0:128] * factors[128:256] * factors[256:384]
    second = factors[384:512] * factors[512:640] * factors[640:768]
    orders = degrees_ref[...]
    left_code = orders[0:1] + 8 * orders[1:2] + 64 * orders[2:3]
    right_code = orders[3:4] + 8 * orders[4:5] + 64 * orders[5:6]
    left = jnp.where(codes_ref[...] == left_code, coeffs_ref[...].reshape(1, -1), 0.0)
    right = jnp.where(codes_ref[...] == right_code, jnp.float32(1.0), 0.0)
    table = high(left, right, ((1,), (1,)))
    trend = jnp.sum(high(table, first, ((0,), (0,))) * second, axis=0, keepdims=True)
    residual = (response_ref[...].reshape(1, rows) - trend).astype(BF16).astype(F32)
    residual8 = jnp.broadcast_to(residual, (8, rows))
    own_res[0] = jnp.zeros((8, 2 * rows), F32)

    @pl.when(core == 0)
    def _():
        own_res[0, :, 0:rows] = residual8

    @pl.when(core == 1)
    def _():
        own_res[0, :, rows : 2 * rows] = residual8

    res_copy = push(own_res.at[0], own_res.at[1], pick_send, pick_recv, sibling)
    for copy in local:
        copy.wait()

    def apply(offset, fresh=False):
        at = on(offset)
        block = cov[:, pl.ds(pl.multiple_of(at * 2 * rows, 128), 2 * rows)]
        for k in (0, 1):
            term = dot(block, panels[k, at])
            lanes = slice(RANK * k, RANK * (k + 1))
            solved_ref[:, lanes] = term if fresh else solved_ref[:, lanes] + term

    res_ring = Ring(
        lambda zz, cc: all_res.at[zz], all_res.at[chip], (4, 3), res_send, res_recv, None, None
    )
    for step in range(1, 5):
        for ring in rings:
            ring.arrive(0, step)
            ring.arrive(1, step)
        if step == 1:
            res_copy.wait_recv()
            all_res[chip] = own_res[0] + own_res[1]
            res_ring.start()
        else:
            res_ring.arrive(0, step - 1)
            res_ring.arrive(1, step - 1)
        for ring in rings:
            ring.handed_over(0, step - 1)
            ring.handed_over(1, step - 1)
        apply(step - 1 if step > 1 else 0, step == 1)
        if step > 1:
            apply(1 - step)
    res_ring.arrive(0, 4)
    for ring in rings:
        ring.handed_over(0, 4)
        ring.handed_over(1, 4)
    apply(4)

    one_t = panels[0, chip, own_rows]
    two_t = panels[1, chip, own_rows]
    upper, lower = split(solved_ref[...])
    inner = ((0,), (0,))
    gram = dot(one_t, upper, inner) + dot(one_t, lower, inner)
    parts[0, :, 0:512] = gram[0:128]
    parts[1, :, 0:384] = gram[128:256, 128:512]
    gram = dot(two_t, upper[:, 256:512], inner) + dot(two_t, lower[:, 256:512], inner)
    parts[0, :, 512:640] = gram[0:128, 128:256]
    parts[0, :, 640:768] = jnp.zeros((HALF, HALF), F32)
    parts[1, :, 512:640] = gram[0:128, 0:128]
    parts[1, :, 640:768] = gram[128:256, 128:256]
    residual_b = residual8.astype(BF16)
    rhs = dot(residual_b, upper) + dot(residual_b, lower)
    line = lax.broadcasted_iota(jnp.int32, (8, HALF), 0)
    packed = jnp.zeros((8, HALF), F32)
    for k in range(4):
        packed = jnp.where(line == k, rhs[:, HALF * k : HALF * (k + 1)], packed)
    parts[1, :, 384:512] = jnp.zeros((HALF, HALF), F32)
    parts[1, 0:8, 384:512] = packed

    swap = push(parts.at[1 - core], from_core, sum_send, sum_recv, sibling)

    def residue(zz, total):
        lanes = pl.ds(pl.multiple_of(zz * 2 * rows, 128), 2 * rows)
        return total + dot(all_res[zz].astype(BF16), cov[:, lanes], ((1,), (1,)))

    residue_ref[...] = lax.fori_loop(0, CHIPS, residue, jnp.zeros((8, rows), F32))
    swap.wait_recv()
    for k in range(CHIPS):
        band = slice(16 * k, 16 * (k + 1))
        mine[k] = parts[core, band] + from_core[band]

    copies = [
        push(
            mine.at[on(o)], from_chips.at[o - 1], chip_send.at[o - 1], chip_recv.at[o - 1],
            chip_at(o),
        )
        for o in range(1, CHIPS)
    ]
    total = mine[chip]
    for o in range(1, CHIPS):
        copies[o - 1].wait_recv()
        total = total + from_chips[o - 1]
    leaf_sum[...] = total

    copies = [
        push(leaf_sum, from_leaves.at[b - 1], leaf_send.at[b - 1], leaf_recv.at[b - 1], leaf_at(b))
        for b in (1, 2, 3)
    ]
    copies[0].wait_recv()
    near = total + from_leaves[0]
    copies[1].wait_recv()
    copies[2].wait_recv()
    far = from_leaves[1] + from_leaves[2]
    grams_ref[0, chip, core, :, 0:512] = near[:, 0:512]
    grams_ref[1, chip, core, :, 0:512] = far[:, 0:512]
    grams_ref[0, chip, core, :, 512:640] = near[:, 512:640] + far[:, 512:640]
    grams_ref[1, chip, core, :, 512:640] = near[:, 640:768] + far[:, 640:768]

    rings = [
        Ring(
            lambda zz, cc, k=k: grams_ref.at[k, zz, cc], grams_ref.at[k, chip, core],
            (4 - k, 3 + k), gram_send.at[k], gram_recv.at[k], pair_send.at[k], pair_recv.at[k],
        )
        for k in (0, 1)
    ]
    for ring in rings:
        ring.start()
    for step in range(1, 5):
        for ring in rings:
            ring.arrive(0, step)
            ring.arrive(1, step)
    for ring in rings:
        for step in range(0, 5):
            ring.handed_over(0, step)
            ring.handed_over(1, step)
    for copy in sent:
        copy.wait_send()


def inverse_of(value):
    guess = pl.reciprocal(value, approx=True)
    guess = guess * (2.0 - value * guess)
    return guess * (2.0 - value * guess)


def root_inverse(value):
    guess = lax.rsqrt(value)
    return guess * (1.5 - 0.5 * value * guess * guess)


def factor(matrices):
    count = len(matrices)
    tile = (count, 8, HALF)
    left = jnp.stack(matrices).reshape(count, 16, 8, HALF)
    lane = lax.broadcasted_iota(jnp.int32, tile, 2)
    line = lax.broadcasted_iota(jnp.int32, tile, 1)
    done = []
    for group in range(16):
        start = 8 * group
        top, left = left[:, 0], left[:, 1:]
        inside = (lane >= start) & (lane < start + 8)
        rows = [jnp.broadcast_to(top[:, j : j + 1], tile) for j in range(8)]
        p = {
            (i, j): jnp.broadcast_to(rows[i][:, :, start + j : start + j + 1], tile)
            for i in range(8)
            for j in range(i, 8)
        }
        rows = [
            jnp.where(inside, jnp.where(lane == start + j, 1.0, 0.0), rows[j]) for j in range(8)
        ]
        ties, scaled, final = [], [None] * 8, [None] * 8
        for i in range(0, 8, 2):
            a, b, d = p[i, i], p[i, i + 1], p[i + 1, i + 1]
            scale = inverse_of(a * d - b * b)
            i00, i01, i11 = d * scale, -b * scale, a * scale
            tie = {}
            for j in range(i + 2, 8):
                tie[j] = (
                    i00 * p[i, j] + i01 * p[i + 1, j],
                    i01 * p[i, j] + i11 * p[i + 1, j],
                )
            for m in range(i + 2, 8):
                for j in range(m, 8):
                    p[m, j] = p[m, j] - (p[i, m] * tie[j][0] + p[i + 1, m] * tie[j][1])
            for j in range(i + 2, 8):
                rows[j] = rows[j] - (tie[j][0] * rows[i] + tie[j][1] * rows[i + 1])
            scaled[i] = i00 * rows[i] + i01 * rows[i + 1]
            scaled[i + 1] = i01 * rows[i] + i11 * rows[i + 1]
            ties.append(tie)
            unit = root_inverse(a)
            final[i] = rows[i] * unit
            b = b * unit
            final[i + 1] = (rows[i + 1] - b * final[i]) * root_inverse(d - b * b)
        for i in (4, 2, 0):
            for j in range(7, i + 1, -1):
                scaled[i] = scaled[i] - ties[i // 2][j][0] * scaled[j]
                scaled[i + 1] = scaled[i + 1] - ties[i // 2][j][1] * scaled[j]
        whole = final[0]
        for j in range(1, 8):
            whole = jnp.where(line == j, final[j], whole)
        done.append(jnp.where(lane < start + 8, whole, 0.0))
        if group < 15:
            shape = left.shape
            columns = [
                jnp.broadcast_to(left[:, :, :, start + j : start + j + 1], shape)
                for j in range(8)
            ]
            left = jnp.where(inside[:, None], 0.0, left)
            for j in (6, 4, 2, 0):
                left = left - (
                    columns[j] * scaled[j][:, None] + columns[j + 1] * scaled[j + 1][:, None]
                )
    whole = jnp.stack(done, axis=1).reshape(count, HALF, HALF)
    return [whole[k] for k in range(count)]


def symmetric(block):
    return 0.5 * (block + block.T)


def solve_kernel(grams_ref, solved_ref, residue_ref, alpha_ref):
    line = lax.broadcasted_iota(jnp.int32, (HALF, HALF), 0)
    lane = lax.broadcasted_iota(jnp.int32, (HALF, HALF), 1)
    eye = jnp.where(line == lane, jnp.float32(1.0), 0.0)
    inner, outer = ((0,), (0,)), ((1,), (1,))

    def block(k, core, start, stop):
        return grams_ref[k, :, core, :, start:stop].reshape(HALF, stop - start)

    def halves(packed, at):
        return [jnp.broadcast_to(packed[at + k : at + k + 1], (8, HALF)) for k in (0, 1)]

    rhs = [grams_ref[k, 0, 1, 0:8, 384:512] for k in (0, 1)]
    head = factor([eye + symmetric(block(k, 0, 0, 128)) for k in (0, 1)])
    tie = [high(head[k], block(k, 0, 128, 256)) for k in (0, 1)]
    tail = factor(
        [eye + symmetric(block(k, 1, 0, 128)) - high(tie[k], tie[k], inner) for k in (0, 1)]
    )

    cross, answers = [], []
    for k in (0, 1):
        upper = high(head[k], block(k, 0, 256, 512))
        lower = high(tail[k], block(k, 1, 128, 384) - high(tie[k], upper, inner))
        cross += [upper, lower]
        f0, f1 = halves(rhs[k], 0)
        y0 = high(f0, head[k], outer)
        answers += [y0, high(f1 - high(y0, tie[k]), tail[k], outer)]
    near_cross = jnp.concatenate(cross[0:2], axis=0)
    near_answers = jnp.concatenate(answers[0:2], axis=1)
    cross = jnp.concatenate(cross, axis=0)
    answers = jnp.concatenate(answers, axis=1)
    gram = high(cross, cross, inner)
    rest = jnp.concatenate(halves(rhs[0] + rhs[1], 2), axis=1) - high(answers, cross)

    (quad_head,) = factor([eye + symmetric(block(0, 1, 512, 640)) - gram[0:128, 0:128]])
    quad_tie = high(quad_head, block(0, 0, 512, 640) - gram[0:128, 128:256])
    (quad_tail,) = factor(
        [
            eye + symmetric(block(1, 1, 512, 640)) - gram[128:256, 128:256]
            - high(quad_tie, quad_tie, inner)
        ]
    )
    y0 = high(rest[:, 0:128], quad_head, outer)
    y1 = high(rest[:, 128:256] - high(y0, quad_tie), quad_tail, outer)

    def back(y0, y1, first, mid, last):
        x1 = high(y1, last)
        return [high(y0 - high(x1, mid, outer), first), x1]

    gain = back(y0, y1, quad_head, quad_tie, quad_tail)
    y = near_answers - high(jnp.concatenate(gain, axis=1), near_cross, outer)
    shift = back(y[:, 0:128], y[:, 128:256], head[0], tie[0], tail[0])
    both = jnp.concatenate(shift + gain, axis=1)
    alpha = residue_ref[...] - high(both, solved_ref[...], outer)
    alpha_ref[...] = alpha[0]


def per_device(inverse_cov, panel_one, panel_two, response, inputs, coeffs, degrees):
    codes, picks = degree_tables()
    rows = panel_one.shape[0]
    vmem = pl.BlockSpec(memory_space=pltpu.VMEM)
    hbm = pl.BlockSpec(memory_space=pltpu.HBM)
    dma = pltpu.SemaphoreType.DMA
    grams, solved, residue = pl.pallas_call(
        gather_kernel,
        out_shape=(
            jax.ShapeDtypeStruct((2, CHIPS, 2, 16, PART), F32),
            jax.ShapeDtypeStruct((rows, 2 * RANK), F32),
            jax.ShapeDtypeStruct((8, rows), F32),
        ),
        in_specs=[hbm] * 9,
        out_specs=(vmem, vmem, vmem),
        scratch_shapes=[
            pltpu.VMEM(response.shape, F32),
            pltpu.VMEM(inputs.shape, F32),
            pltpu.VMEM(coeffs.shape, F32),
            pltpu.VMEM(degrees.shape, jnp.int32),
            pltpu.VMEM(codes.shape, jnp.int32),
            pltpu.VMEM(picks.shape, F32),
            pltpu.VMEM(inverse_cov.shape, BF16),
            pltpu.VMEM((2, CHIPS, 2 * rows, RANK), BF16),
            pltpu.VMEM((8, rows), F32),
            pltpu.VMEM((2, 8, 2 * rows), F32),
            pltpu.VMEM((CHIPS, 8, 2 * rows), F32),
            pltpu.VMEM((2, HALF, WIDE), F32),
            pltpu.VMEM((HALF, WIDE), F32),
            pltpu.VMEM((CHIPS, 16, WIDE), F32),
            pltpu.VMEM((CHIPS - 1, 16, WIDE), F32),
            pltpu.VMEM((16, WIDE), F32),
            pltpu.VMEM((3, 16, WIDE), F32),
            dma((9,)),
            dma((2, 2, 4)), dma((2, 2, 4)),
            dma((2, 9)), dma((2, 9)),
            dma((2, 4)), dma((2, 4)),
            dma, dma,
            dma, dma,
            dma((CHIPS - 1,)), dma((CHIPS - 1,)),
            dma((3,)), dma((3,)),
            dma((2, 2, 4)), dma((2, 2, 4)),
            dma((2, 9)), dma((2, 9)),
        ],
        compiler_params=pltpu.CompilerParams(
            collective_id=0, has_side_effects=True, vmem_limit_bytes=63 * 1024 * 1024
        ),
    )(
        inverse_cov, panel_one, panel_two, response, inputs, coeffs, degrees, jnp.asarray(codes), jnp.asarray(picks),
    )
    alpha = pl.pallas_call(
        solve_kernel,
        out_shape=jax.ShapeDtypeStruct((rows,), F32),
        in_specs=[vmem] * 3,
        out_specs=vmem,
        compiler_params=pltpu.CompilerParams(vmem_limit_bytes=63 * 1024 * 1024),
    )(grams, solved, residue)
    return alpha


def solution(mesh):
    in_specs = (
        P(("runs", "rank"), None),
        P(("runs", "rank"), None),
        P(("runs", "rank"), None),
        P(("runs", "rank")),
        P(None, ("runs", "rank")),
        P(),
        P(),
    )
    out_specs = P(("runs", "rank"))
    return jax.shard_map(
        per_device, mesh=mesh, in_specs=in_specs, out_specs=out_specs, check_vma=False
    )
```

```python
import math

import jax
import jax.numpy as jnp
import numpy as np
from jax import lax
from jax.experimental import pallas as pl
from jax.experimental.pallas import tpu as pltpu
from jax.sharding import PartitionSpec as P

MESH = pl.DeviceIdType.MESH
F32 = jnp.float32
BF16 = jnp.bfloat16
HIGHEST = lax.Precision.HIGHEST
RANK = 256
HALF = 128
CHIPS = 8


def degree_tables():
    triples = [
        (a, b, c) for a in range(8) for b in range(8) for c in range(8) if a + b + c <= 7
    ]
    codes = np.full((HALF, 1), -1, np.int32)
    picks = np.zeros((6, HALF, 64), np.float32)
    for row, triple in enumerate(triples):
        codes[row, 0] = triple[0] + 8 * triple[1] + 64 * triple[2]
        for column in range(6):
            picks[column, row, triple[column % 3] * 8 + column] = 1.0
    return codes, picks.reshape(6 * HALF, 64)


def dot(left, right, dims=((1,), (0,)), precision=None):
    return lax.dot_general(
        left, right, (dims, ((), ())), precision=precision, preferred_element_type=F32
    )


def high(left, right, dims=((1,), (0,))):
    return dot(left, right, dims, HIGHEST)


def split(value):
    upper = value.astype(BF16)
    return upper, (value - upper.astype(F32)).astype(BF16)


def gather_kernel(
    cov_ref, one_ref, two_ref, response_hbm, inputs_hbm, coeffs_hbm, degrees_hbm, codes_hbm,
    picks_hbm, grams_ref, quad_ref, solved_ref, residue_ref,
    response_ref, inputs_ref, coeffs_ref, degrees_ref, codes_ref, picks_ref, cov, panels,
    points, own_res, all_res, pair_parts, quad_parts, local_sem, panel_send, panel_recv, core_send,
    core_recv, res_send, res_recv, pick_send, pick_recv, pair_bufs, quad_bufs, gram_sems, last_sems,
):
    leaf = lax.axis_index("runs")
    place = lax.axis_index("rank")
    chip, core = place // 2, place % 2
    rows = one_ref.shape[0]
    own_rows = pl.ds(pl.multiple_of(core * rows, 64), rows)

    def on(offset):
        return lax.rem(chip + offset + CHIPS, CHIPS)

    def chip_at(offset):
        return (leaf, 2 * on(offset) + core)

    sibling = (leaf, 2 * chip + 1 - core)

    def leaf_at(bits):
        return (leaf ^ bits, place)

    peers = [chip_at(o) for o in range(1, CHIPS)] + [sibling] + [leaf_at(b) for b in (1, 2, 3)]
    barrier = pltpu.get_barrier_semaphore()
    for peer in peers:
        pl.semaphore_signal(barrier, inc=1, device_id=peer, device_id_type=MESH)

    operands = (one_ref, two_ref)
    local = [
        pltpu.make_async_copy(one_ref, panels.at[0, chip, own_rows], local_sem.at[0]),
        pltpu.make_async_copy(two_ref, panels.at[1, chip, own_rows], local_sem.at[1]),
        pltpu.make_async_copy(cov_ref, cov, local_sem.at[2]),
    ]
    small = [
        pltpu.make_async_copy(src, dst, local_sem.at[3 + k])
        for k, (src, dst) in enumerate(
            [
                (response_hbm, response_ref), (inputs_hbm, inputs_ref), (coeffs_hbm, coeffs_ref),
                (degrees_hbm, degrees_ref), (codes_hbm, codes_ref), (picks_hbm, picks_ref),
            ]
        )
    ]
    for copy in small:
        copy.start()
    for copy in local:
        copy.start()
    pl.semaphore_wait(barrier, len(peers))

    sent = []

    def push(src, dst, send, recv, device):
        copy = pltpu.make_async_remote_copy(
            src_ref=src, dst_ref=dst, send_sem=send, recv_sem=recv, device_id=device,
            device_id_type=MESH,
        )
        copy.start()
        sent.append(copy)
        return copy

    class Ring:
        def __init__(self, view, own, steps, send, recv, core_sends, core_recvs):
            self.view, self.own, self.steps = view, own, steps
            self.send, self.recv = send, recv
            self.core_sends, self.core_recvs = core_sends, core_recvs
            self.flying, self.handed = {}, {}

        def forward(self, way, step, src):
            offset = -(step - 1) if way == 0 else step - 1
            self.flying[way, step] = push(
                src, self.view(on(offset), core), self.send.at[way, step - 1],
                self.recv.at[way, step - 1], chip_at(1 if way == 0 else -1),
            )

        def hand(self, way, step, src):
            offset = -step if way == 0 else step
            slot = 4 * way + step
            self.handed[way, step] = push(
                src, self.view(on(offset), core), self.core_sends.at[slot],
                self.core_recvs.at[slot], sibling,
            )

        def start(self):
            for way in (0, 1):
                self.forward(way, 1, self.own)
            if self.core_sends is not None:
                self.hand(0, 0, self.own)

        def arrive(self, way, step):
            if step > self.steps[way]:
                return
            self.flying[way, step].wait_recv()
            block = self.view(on(-step if way == 0 else step), core)
            if step < self.steps[way]:
                self.forward(way, step + 1, block)
            if self.core_sends is not None:
                self.hand(way, step, block)

        def handed_over(self, way, step):
            if (way, step) in self.handed:
                self.handed[way, step].wait_recv()

    half = rows // 2

    def panel_view(k, h):
        return lambda zz, cc: panels.at[k, zz, pl.ds(pl.multiple_of(cc * rows + h * half, 32), half)]

    panel_rings = [
        [
            Ring(
                panel_view(k, h), operands[k].at[pl.ds(h * half, half)], (4 - h, 3 + h),
                panel_send.at[2 * k + h], panel_recv.at[2 * k + h], core_send.at[2 * k + h],
                core_recv.at[2 * k + h],
            )
            for h in (0, 1)
        ]
        for k in (0, 1)
    ]
    for ring in panel_rings[0]:
        ring.start()

    for copy in small:
        copy.wait()
    points[...] = jnp.zeros(points.shape, F32)
    points[0:6, :] = inputs_ref[...]
    x = points[...]
    levels = [jnp.ones_like(x), x]
    for k in range(1, 7):
        levels.append(((2 * k + 1) * x * levels[k] - k * levels[k - 1]) / (k + 1))
    levels = [math.sqrt(2 * k + 1) * level for k, level in enumerate(levels)]
    factors = high(picks_ref[...], jnp.concatenate(levels, axis=0))
    first = factors[0:128] * factors[128:256] * factors[256:384]
    second = factors[384:512] * factors[512:640] * factors[640:768]
    orders = degrees_ref[...]
    left_code = orders[0:1] + 8 * orders[1:2] + 64 * orders[2:3]
    right_code = orders[3:4] + 8 * orders[4:5] + 64 * orders[5:6]
    left = jnp.where(codes_ref[...] == left_code, coeffs_ref[...].reshape(1, -1), 0.0)
    right = jnp.where(codes_ref[...] == right_code, jnp.float32(1.0), 0.0)
    table = high(left, right, ((1,), (1,)))
    trend = jnp.sum(high(table, first, ((0,), (0,))) * second, axis=0, keepdims=True)
    residual = (response_ref[...].reshape(1, rows) - trend).astype(BF16).astype(F32)
    residual8 = jnp.broadcast_to(residual, (8, rows))
    own_res[0] = jnp.zeros((8, 2 * rows), F32)

    @pl.when(core == 0)
    def _():
        own_res[0, :, 0:rows] = residual8

    @pl.when(core == 1)
    def _():
        own_res[0, :, rows : 2 * rows] = residual8

    res_copy = push(own_res.at[0], own_res.at[1], pick_send, pick_recv, sibling)
    for copy in local:
        copy.wait()

    def apply(k, offset, fresh=False):
        at = on(offset)
        block = cov[:, pl.ds(pl.multiple_of(at * 2 * rows, 128), 2 * rows)]
        term = dot(block, panels[k, at])
        lanes = slice(RANK * k, RANK * (k + 1))
        solved_ref[:, lanes] = term if fresh else solved_ref[:, lanes] + term

    def serve(rings, step):
        for ring in rings:
            ring.arrive(0, step)
            ring.arrive(1, step)

    def handed(rings, step):
        for ring in rings:
            ring.handed_over(0, step)
            ring.handed_over(1, step)

    def absorb(k, step):
        handed(panel_rings[k], step)
        apply(k, step, step == 0)
        if 0 < step < 4:
            apply(k, -step)

    class Total:
        def __init__(self, parts, bufs):
            self.parts = parts
            (self.from_core, self.mine, self.from_chips, self.leaf_sum, self.from_leaves) = bufs[0:5]
            (self.sum_sem, self.chip_sem, self.leaf_sem) = bufs[5:8]

        def swap(self):
            self.swapped = push(
                self.parts.at[1 - core], self.from_core, self.sum_sem.at[0], self.sum_sem.at[1],
                sibling,
            )

        def spread(self):
            self.swapped.wait_recv()
            for k in range(CHIPS):
                band = slice(16 * k, 16 * (k + 1))
                self.mine[k] = self.parts[core, band] + self.from_core[band]
            self.copies = [
                push(
                    self.mine.at[on(o)], self.from_chips.at[o - 1], self.chip_sem.at[0, o - 1],
                    self.chip_sem.at[1, o - 1], chip_at(o),
                )
                for o in range(1, CHIPS)
            ]

        def cross(self):
            self.total = self.mine[chip]
            for o in range(1, CHIPS):
                self.copies[o - 1].wait_recv()
                self.total = self.total + self.from_chips[o - 1]
            self.leaf_sum[...] = self.total
            self.copies = [
                push(
                    self.leaf_sum, self.from_leaves.at[b - 1], self.leaf_sem.at[0, b - 1],
                    self.leaf_sem.at[1, b - 1], leaf_at(b),
                )
                for b in (1, 2, 3)
            ]

        def finish(self):
            self.copies[0].wait_recv()
            near = self.leaf_sum[...] + self.from_leaves[0]
            self.copies[1].wait_recv()
            self.copies[2].wait_recv()
            return near, self.from_leaves[1] + self.from_leaves[2]

    def gram_rings(ref, sems):
        return [
            Ring(
                lambda zz, cc, k=k: ref.at[k, zz, cc], ref.at[k, chip, core], (4 - k, 3 + k),
                sems[0].at[k], sems[1].at[k], sems[2].at[k], sems[3].at[k],
            )
            for k in (0, 1)
        ]

    pair_total, quad_total = Total(pair_parts, pair_bufs), Total(quad_parts, quad_bufs)
    pair_rings, quad_rings = gram_rings(grams_ref, gram_sems), gram_rings(quad_ref, last_sems)
    residual_b = residual8.astype(BF16)
    inner = ((0,), (0,))
    line = lax.broadcasted_iota(jnp.int32, (8, HALF), 0)

    def terms(k, blocks):
        upper, lower = split(solved_ref[:, RANK * k : RANK * (k + 1)])
        gram = dot(upper, blocks, inner) + dot(lower, blocks, inner)
        rhs = dot(residual_b, upper) + dot(residual_b, lower)
        lines = jnp.where(line == 0, rhs[:, 0:HALF], jnp.where(line == 1, rhs[:, HALF:], 0.0))
        return gram, lines

    res_ring = Ring(
        lambda zz, cc: all_res.at[zz], all_res.at[chip], (4, 3), res_send, res_recv, None, None
    )
    for step in range(1, 5):
        serve(panel_rings[0], step)
        if step == 1:
            res_copy.wait_recv()
            all_res[chip] = own_res[0] + own_res[1]
            res_ring.start()
        else:
            serve([res_ring], step - 1)
        if step == 3:
            for ring in panel_rings[1]:
                ring.start()
        absorb(0, step - 1)
    absorb(0, 4)

    own_one = panels[0, chip, own_rows]
    own_two = panels[1, chip, own_rows]
    gram, lines = terms(0, jnp.concatenate([own_one, own_two], axis=1))
    pair_parts[0] = gram[0:128]
    pair_parts[1, :, 0:384] = gram[128:256, 128:512]
    pair_parts[1, :, 384:512] = jnp.zeros((HALF, HALF), F32)
    pair_parts[1, 0:8, 384:512] = lines
    pair_total.swap()
    serve(panel_rings[1], 1)
    absorb(1, 0)
    pair_total.spread()
    serve(panel_rings[1], 2)
    absorb(1, 1)
    pair_total.cross()
    serve(panel_rings[1], 3)
    serve([res_ring], 4)
    absorb(1, 2)
    grams_ref[0, chip, core], grams_ref[1, chip, core] = pair_total.finish()
    for ring in pair_rings:
        ring.start()
    serve(panel_rings[1], 4)
    absorb(1, 3)
    serve(pair_rings, 1)
    absorb(1, 4)

    gram, lines = terms(1, own_two)
    quad_parts[0, :, 0:128] = gram[0:128, 128:256]
    quad_parts[0, :, 128:256] = jnp.zeros((HALF, HALF), F32)
    quad_parts[0, 0:8, 128:256] = lines
    quad_parts[1, :, 0:128] = gram[0:128, 0:128]
    quad_parts[1, :, 128:256] = gram[128:256, 128:256]
    quad_total.swap()
    serve(pair_rings, 2)
    quad_total.spread()
    serve(pair_rings, 3)

    def residue(zz, total):
        lanes = pl.ds(pl.multiple_of(zz * 2 * rows, 128), 2 * rows)
        return total + dot(all_res[zz].astype(BF16), cov[:, lanes], ((1,), (1,)))

    residue_ref[...] = lax.fori_loop(0, CHIPS, residue, jnp.zeros((8, rows), F32))
    quad_total.cross()
    serve(pair_rings, 4)
    near, far = quad_total.finish()
    total = near + far
    quad_ref[0, chip, core] = total[:, 0:128]
    quad_ref[1, chip, core] = total[:, 128:256]
    for ring in quad_rings:
        ring.start()
    for step in range(1, 5):
        serve(quad_rings, step)
    for step in range(0, 5):
        handed(pair_rings, step)
        handed(quad_rings, step)
    for copy in sent:
        copy.wait_send()


def inverse_of(value):
    guess = pl.reciprocal(value, approx=True)
    guess = guess * (2.0 - value * guess)
    return guess * (2.0 - value * guess)


def root_inverse(value):
    guess = lax.rsqrt(value)
    return guess * (1.5 - 0.5 * value * guess * guess)


def factor(matrices):
    count = len(matrices)
    tile = (count, 8, HALF)
    left = jnp.stack(matrices).reshape(count, 16, 8, HALF)
    lane = lax.broadcasted_iota(jnp.int32, tile, 2)
    line = lax.broadcasted_iota(jnp.int32, tile, 1)
    done = []
    for group in range(16):
        start = 8 * group
        top, left = left[:, 0], left[:, 1:]
        inside = (lane >= start) & (lane < start + 8)
        rows = [jnp.broadcast_to(top[:, j : j + 1], tile) for j in range(8)]
        p = {
            (i, j): jnp.broadcast_to(rows[i][:, :, start + j : start + j + 1], tile)
            for i in range(8)
            for j in range(i, 8)
        }
        rows = [
            jnp.where(inside, jnp.where(lane == start + j, 1.0, 0.0), rows[j]) for j in range(8)
        ]
        ties, scaled, final = [], [None] * 8, [None] * 8
        for i in range(0, 8, 2):
            a, b, d = p[i, i], p[i, i + 1], p[i + 1, i + 1]
            scale = inverse_of(a * d - b * b)
            i00, i01, i11 = d * scale, -b * scale, a * scale
            tie = {}
            for j in range(i + 2, 8):
                tie[j] = (
                    i00 * p[i, j] + i01 * p[i + 1, j],
                    i01 * p[i, j] + i11 * p[i + 1, j],
                )
            for m in range(i + 2, 8):
                for j in range(m, 8):
                    p[m, j] = p[m, j] - (p[i, m] * tie[j][0] + p[i + 1, m] * tie[j][1])
            for j in range(i + 2, 8):
                rows[j] = rows[j] - (tie[j][0] * rows[i] + tie[j][1] * rows[i + 1])
            scaled[i] = i00 * rows[i] + i01 * rows[i + 1]
            scaled[i + 1] = i01 * rows[i] + i11 * rows[i + 1]
            ties.append(tie)
            unit = root_inverse(a)
            final[i] = rows[i] * unit
            b = b * unit
            final[i + 1] = (rows[i + 1] - b * final[i]) * root_inverse(d - b * b)
        for i in (4, 2, 0):
            for j in range(7, i + 1, -1):
                scaled[i] = scaled[i] - ties[i // 2][j][0] * scaled[j]
                scaled[i + 1] = scaled[i + 1] - ties[i // 2][j][1] * scaled[j]
        whole = final[0]
        for j in range(1, 8):
            whole = jnp.where(line == j, final[j], whole)
        done.append(jnp.where(lane < start + 8, whole, 0.0))
        if group < 15:
            shape = left.shape
            columns = [
                jnp.broadcast_to(left[:, :, :, start + j : start + j + 1], shape)
                for j in range(8)
            ]
            left = jnp.where(inside[:, None], 0.0, left)
            for j in (6, 4, 2, 0):
                left = left - (
                    columns[j] * scaled[j][:, None] + columns[j + 1] * scaled[j + 1][:, None]
                )
    whole = jnp.stack(done, axis=1).reshape(count, HALF, HALF)
    return [whole[k] for k in range(count)]


def symmetric(block):
    return 0.5 * (block + block.T)


def solve_kernel(grams_ref, quad_ref, solved_ref, residue_ref, alpha_ref):
    line = lax.broadcasted_iota(jnp.int32, (HALF, HALF), 0)
    lane = lax.broadcasted_iota(jnp.int32, (HALF, HALF), 1)
    eye = jnp.where(line == lane, jnp.float32(1.0), 0.0)
    inner, outer = ((0,), (0,)), ((1,), (1,))

    def block(k, core, start, stop):
        return grams_ref[k, :, core, :, start:stop].reshape(HALF, stop - start)

    def quad_block(k, core):
        return quad_ref[k, :, core].reshape(HALF, HALF)

    def halves(packed):
        return [jnp.broadcast_to(packed[k : k + 1], (8, HALF)) for k in (0, 1)]

    rhs = [grams_ref[k, 0, 1, 0:8, 384:512] for k in (0, 1)]
    head = factor([eye + symmetric(block(k, 0, 0, 128)) for k in (0, 1)])
    tie = [high(head[k], block(k, 0, 128, 256)) for k in (0, 1)]
    tail = factor(
        [eye + symmetric(block(k, 1, 0, 128)) - high(tie[k], tie[k], inner) for k in (0, 1)]
    )

    cross, answers = [], []
    for k in (0, 1):
        upper = high(head[k], block(k, 0, 256, 512))
        lower = high(tail[k], block(k, 1, 128, 384) - high(tie[k], upper, inner))
        cross += [upper, lower]
        f0, f1 = halves(rhs[k])
        y0 = high(f0, head[k], outer)
        answers += [y0, high(f1 - high(y0, tie[k]), tail[k], outer)]
    near_cross = jnp.concatenate(cross[0:2], axis=0)
    near_answers = jnp.concatenate(answers[0:2], axis=1)
    cross = jnp.concatenate(cross, axis=0)
    answers = jnp.concatenate(answers, axis=1)
    gram = high(cross, cross, inner)
    rest = jnp.concatenate(halves(quad_ref[1, 0, 0, 0:8]), axis=1) - high(answers, cross)

    (quad_head,) = factor([eye + symmetric(quad_block(0, 1)) - gram[0:128, 0:128]])
    quad_tie = high(quad_head, quad_block(0, 0) - gram[0:128, 128:256])
    (quad_tail,) = factor(
        [
            eye + symmetric(quad_block(1, 1)) - gram[128:256, 128:256]
            - high(quad_tie, quad_tie, inner)
        ]
    )
    y0 = high(rest[:, 0:128], quad_head, outer)
    y1 = high(rest[:, 128:256] - high(y0, quad_tie), quad_tail, outer)

    def back(y0, y1, first, mid, last):
        x1 = high(y1, last)
        return [high(y0 - high(x1, mid, outer), first), x1]

    gain = back(y0, y1, quad_head, quad_tie, quad_tail)
    y = near_answers - high(jnp.concatenate(gain, axis=1), near_cross, outer)
    shift = back(y[:, 0:128], y[:, 128:256], head[0], tie[0], tail[0])
    both = jnp.concatenate(shift + gain, axis=1)
    alpha = residue_ref[...] - high(both, solved_ref[...], outer)
    alpha_ref[...] = alpha[0]


def per_device(inverse_cov, panel_one, panel_two, response, inputs, coeffs, degrees):
    codes, picks = degree_tables()
    rows = panel_one.shape[0]
    vmem = pl.BlockSpec(memory_space=pltpu.VMEM)
    hbm = pl.BlockSpec(memory_space=pltpu.HBM)
    dma = pltpu.SemaphoreType.DMA

    def sum_buffers(wide):
        return (
            pltpu.VMEM((HALF, wide), F32),
            pltpu.VMEM((CHIPS, 16, wide), F32),
            pltpu.VMEM((CHIPS - 1, 16, wide), F32),
            pltpu.VMEM((16, wide), F32),
            pltpu.VMEM((3, 16, wide), F32),
            dma((2,)), dma((2, CHIPS - 1)), dma((2, 3)),
        )

    ring_sems = (dma((2, 2, 4)), dma((2, 2, 4)), dma((2, 9)), dma((2, 9)))
    grams, quads, solved, residue = pl.pallas_call(
        gather_kernel,
        out_shape=(
            jax.ShapeDtypeStruct((2, CHIPS, 2, 16, 512), F32),
            jax.ShapeDtypeStruct((2, CHIPS, 2, 16, 128), F32),
            jax.ShapeDtypeStruct((rows, 2 * RANK), F32),
            jax.ShapeDtypeStruct((8, rows), F32),
        ),
        in_specs=[hbm] * 9,
        out_specs=(vmem,) * 4,
        scratch_shapes=[
            pltpu.VMEM(response.shape, F32),
            pltpu.VMEM(inputs.shape, F32),
            pltpu.VMEM(coeffs.shape, F32),
            pltpu.VMEM(degrees.shape, jnp.int32),
            pltpu.VMEM(codes.shape, jnp.int32),
            pltpu.VMEM(picks.shape, F32),
            pltpu.VMEM(inverse_cov.shape, BF16),
            pltpu.VMEM((2, CHIPS, 2 * rows, RANK), BF16),
            pltpu.VMEM((8, rows), F32),
            pltpu.VMEM((2, 8, 2 * rows), F32),
            pltpu.VMEM((CHIPS, 8, 2 * rows), F32),
            pltpu.VMEM((2, HALF, 512), F32),
            pltpu.VMEM((2, HALF, 256), F32),
            dma((9,)),
            dma((4, 2, 4)), dma((4, 2, 4)),
            dma((4, 9)), dma((4, 9)),
            dma((2, 4)), dma((2, 4)),
            dma, dma,
            sum_buffers(512), sum_buffers(256),
            ring_sems, ring_sems,
        ],
        compiler_params=pltpu.CompilerParams(
            collective_id=0, has_side_effects=True, vmem_limit_bytes=63 * 1024 * 1024
        ),
    )(
        inverse_cov, panel_one, panel_two, response, inputs, coeffs, degrees,
        jnp.asarray(codes), jnp.asarray(picks),
    )
    alpha = pl.pallas_call(
        solve_kernel,
        out_shape=jax.ShapeDtypeStruct((rows,), F32),
        in_specs=[vmem] * 4,
        out_specs=vmem,
        compiler_params=pltpu.CompilerParams(vmem_limit_bytes=63 * 1024 * 1024),
    )(grams, quads, solved, residue)
    return alpha


def solution(mesh):
    in_specs = (
        P(("runs", "rank"), None),
        P(("runs", "rank"), None),
        P(("runs", "rank"), None),
        P(("runs", "rank")),
        P(None, ("runs", "rank")),
        P(),
        P(),
    )
    out_specs = P(("runs", "rank"))
    return jax.shard_map(
        per_device, mesh=mesh, in_specs=in_specs, out_specs=out_specs, check_vma=False
    )
```

```python
import math

import jax
import jax.numpy as jnp
import numpy as np
from jax import lax
from jax.experimental import pallas as pl
from jax.experimental.pallas import tpu as pltpu
from jax.sharding import PartitionSpec as P

MESH = pl.DeviceIdType.MESH
F32 = jnp.float32
BF16 = jnp.bfloat16
HIGHEST = lax.Precision.HIGHEST
RANK = 256
HALF = 128
CHIPS = 8


def degree_tables():
    triples = [
        (a, b, c) for a in range(8) for b in range(8) for c in range(8) if a + b + c <= 7
    ]
    codes = np.full((HALF, 1), -1, np.int32)
    picks = np.zeros((6, HALF, 64), np.float32)
    for row, triple in enumerate(triples):
        codes[row, 0] = triple[0] + 8 * triple[1] + 64 * triple[2]
        for column in range(6):
            picks[column, row, triple[column % 3] * 8 + column] = 1.0
    return codes, np.tile(picks.reshape(6 * HALF, 64), (1, 3)).astype(jnp.bfloat16)


def dot(left, right, dims=((1,), (0,)), precision=None):
    return lax.dot_general(
        left, right, (dims, ((), ())), precision=precision, preferred_element_type=F32
    )


def high(left, right, dims=((1,), (0,))):
    return dot(left, right, dims, HIGHEST)


def pieces(value):
    parts = []
    for _ in range(3):
        parts.append(value.astype(BF16))
        value = value - parts[-1].astype(F32)
    return parts


def split(value):
    upper = value.astype(BF16)
    return upper, (value - upper.astype(F32)).astype(BF16)


def mid(left, right, dims=((1,), (0,))):
    upper, lower = split(right)
    if dims[0] == (0,):
        first, second = split(left)
        return dot(first, upper, dims) + dot(second, upper, dims) + dot(first, lower, dims)
    count = left.shape[0]
    first = left.astype(BF16)
    whole = first.astype(F32)
    both = dot(jnp.concatenate([whole, left - whole], axis=0).astype(BF16), upper, dims)
    return both[:count] + both[count:] + dot(first, lower, dims)


def gather_kernel(
    cov_ref, one_ref, two_ref, response_hbm, inputs_hbm, coeffs_hbm, degrees_hbm, codes_hbm,
    picks_hbm, grams_ref, quad_ref, solved_ref, residue_ref,
    response_ref, inputs_ref, coeffs_ref, degrees_ref, codes_ref, picks_ref, cov, panels,
    points, own_res, all_res, pair_parts, quad_parts, local_sem, panel_send, panel_recv, core_send,
    core_recv, res_send, res_recv, pick_send, pick_recv, pair_bufs, quad_bufs, gram_sems, last_sems,
):
    leaf = lax.axis_index("runs")
    place = lax.axis_index("rank")
    chip, core = place // 2, place % 2
    rows = one_ref.shape[0]
    own_rows = pl.ds(pl.multiple_of(core * rows, 64), rows)

    def on(offset):
        return lax.rem(chip + offset + CHIPS, CHIPS)

    def chip_at(offset):
        return (leaf, 2 * on(offset) + core)

    sibling = (leaf, 2 * chip + 1 - core)

    def leaf_at(bits):
        return (leaf ^ bits, place)

    peers = [chip_at(o) for o in range(1, CHIPS)] + [sibling] + [leaf_at(b) for b in (1, 2, 3)]
    barrier = pltpu.get_barrier_semaphore()
    for peer in peers:
        pl.semaphore_signal(barrier, inc=1, device_id=peer, device_id_type=MESH)

    operands = (one_ref, two_ref)
    local = [
        pltpu.make_async_copy(one_ref, panels.at[0, chip, own_rows], local_sem.at[0]),
        pltpu.make_async_copy(two_ref, panels.at[1, chip, own_rows], local_sem.at[1]),
        pltpu.make_async_copy(cov_ref, cov, local_sem.at[2]),
    ]
    small = [
        pltpu.make_async_copy(src, dst, local_sem.at[3 + k])
        for k, (src, dst) in enumerate(
            [
                (response_hbm, response_ref), (inputs_hbm, inputs_ref), (coeffs_hbm, coeffs_ref),
                (degrees_hbm, degrees_ref), (codes_hbm, codes_ref), (picks_hbm, picks_ref),
            ]
        )
    ]
    for copy in small:
        copy.start()
    for copy in local:
        copy.start()
    pl.semaphore_wait(barrier, len(peers))

    sent = []

    def push(src, dst, send, recv, device):
        copy = pltpu.make_async_remote_copy(
            src_ref=src, dst_ref=dst, send_sem=send, recv_sem=recv, device_id=device,
            device_id_type=MESH,
        )
        copy.start()
        sent.append(copy)
        return copy

    class Ring:
        def __init__(self, view, own, steps, send, recv, core_sends, core_recvs):
            self.view, self.own, self.steps = view, own, steps
            self.send, self.recv = send, recv
            self.core_sends, self.core_recvs = core_sends, core_recvs
            self.flying, self.handed = {}, {}

        def forward(self, way, step, src):
            offset = -(step - 1) if way == 0 else step - 1
            self.flying[way, step] = push(
                src, self.view(on(offset), core), self.send.at[way, step - 1],
                self.recv.at[way, step - 1], chip_at(1 if way == 0 else -1),
            )

        def hand(self, way, step, src):
            offset = -step if way == 0 else step
            slot = 4 * way + step
            self.handed[way, step] = push(
                src, self.view(on(offset), core), self.core_sends.at[slot],
                self.core_recvs.at[slot], sibling,
            )

        def start(self):
            for way in (0, 1):
                self.forward(way, 1, self.own)
            if self.core_sends is not None:
                self.hand(0, 0, self.own)

        def arrive(self, way, step):
            if step > self.steps[way]:
                return
            self.flying[way, step].wait_recv()
            block = self.view(on(-step if way == 0 else step), core)
            if step < self.steps[way]:
                self.forward(way, step + 1, block)
            if self.core_sends is not None:
                self.hand(way, step, block)

        def handed_over(self, way, step):
            if (way, step) in self.handed:
                self.handed[way, step].wait_recv()

    half = rows // 2

    def panel_view(k, h):
        return lambda zz, cc: panels.at[k, zz, pl.ds(pl.multiple_of(cc * rows + h * half, 32), half)]

    panel_rings = [
        [
            Ring(
                panel_view(k, h), operands[k].at[pl.ds(h * half, half)], (4 - h, 3 + h),
                panel_send.at[2 * k + h], panel_recv.at[2 * k + h], core_send.at[2 * k + h],
                core_recv.at[2 * k + h],
            )
            for h in (0, 1)
        ]
        for k in (0, 1)
    ]
    for ring in panel_rings[0] + panel_rings[1]:
        ring.start()

    for copy in small:
        copy.wait()
    points[...] = jnp.zeros(points.shape, F32)
    points[0:6, :] = inputs_ref[...]
    x = points[...]
    levels = [jnp.ones_like(x), x]
    for k in range(1, 7):
        levels.append(((2 * k + 1) * x * levels[k] - k * levels[k - 1]) / (k + 1))
    levels = [math.sqrt(2 * k + 1) * level for k, level in enumerate(levels)]
    factors = dot(picks_ref[...], jnp.concatenate(pieces(jnp.concatenate(levels, axis=0)), axis=0))
    first = factors[0:128] * factors[128:256] * factors[256:384]
    second = factors[384:512] * factors[512:640] * factors[640:768]
    orders = degrees_ref[...]
    left_code = orders[0:1] + 8 * orders[1:2] + 64 * orders[2:3]
    right_code = orders[3:4] + 8 * orders[4:5] + 64 * orders[5:6]
    left = jnp.where(codes_ref[...] == left_code, coeffs_ref[...].reshape(1, -1), 0.0)
    right = jnp.where(codes_ref[...] == right_code, 1.0, 0.0).astype(BF16)
    table = dot(jnp.concatenate(pieces(left), axis=0), right, ((1,), (1,)))
    table = table[0:128] + table[128:256] + table[256:384]
    trend = jnp.sum(high(table, first, ((0,), (0,))) * second, axis=0, keepdims=True)
    residual = (response_ref[...].reshape(1, rows) - trend).astype(BF16).astype(F32)
    residual8 = jnp.broadcast_to(residual, (8, rows))
    own_res[0] = jnp.zeros((8, 2 * rows), F32)

    @pl.when(core == 0)
    def _():
        own_res[0, :, 0:rows] = residual8

    @pl.when(core == 1)
    def _():
        own_res[0, :, rows : 2 * rows] = residual8

    res_copy = push(own_res.at[0], own_res.at[1], pick_send, pick_recv, sibling)
    for copy in local:
        copy.wait()

    def apply(k, offset, fresh=False):
        at = on(offset)
        block = cov[:, pl.ds(pl.multiple_of(at * 2 * rows, 128), 2 * rows)]
        term = dot(block, panels[k, at])
        lanes = slice(RANK * k, RANK * (k + 1))
        solved_ref[:, lanes] = term if fresh else solved_ref[:, lanes] + term

    def serve(rings, step):
        for ring in rings:
            ring.arrive(0, step)
            ring.arrive(1, step)

    def handed(rings, step):
        for ring in rings:
            ring.handed_over(0, step)
            ring.handed_over(1, step)

    def absorb(k, step):
        handed(panel_rings[k], step)
        apply(k, step, step == 0)
        if 0 < step < 4:
            apply(k, -step)

    class Total:
        def __init__(self, parts, bufs):
            self.parts = parts
            (self.from_core, self.mine, self.from_chips, self.leaf_sum, self.from_leaves) = bufs[0:5]
            (self.sum_sem, self.chip_sem, self.leaf_sem) = bufs[5:8]

        def swap(self):
            self.swapped = push(
                self.parts.at[1 - core], self.from_core, self.sum_sem.at[0], self.sum_sem.at[1],
                sibling,
            )

        def spread(self):
            self.swapped.wait_recv()
            for k in range(CHIPS):
                band = slice(16 * k, 16 * (k + 1))
                self.mine[k] = self.parts[core, band] + self.from_core[band]
            self.copies = [
                push(
                    self.mine.at[on(o)], self.from_chips.at[o - 1], self.chip_sem.at[0, o - 1],
                    self.chip_sem.at[1, o - 1], chip_at(o),
                )
                for o in range(1, CHIPS)
            ]

        def cross(self):
            self.total = self.mine[chip]
            for o in range(1, CHIPS):
                self.copies[o - 1].wait_recv()
                self.total = self.total + self.from_chips[o - 1]
            self.leaf_sum[...] = self.total
            self.copies = [
                push(
                    self.leaf_sum, self.from_leaves.at[b - 1], self.leaf_sem.at[0, b - 1],
                    self.leaf_sem.at[1, b - 1], leaf_at(b),
                )
                for b in (1, 2, 3)
            ]

        def finish(self):
            self.copies[0].wait_recv()
            near = self.leaf_sum[...] + self.from_leaves[0]
            self.copies[1].wait_recv()
            self.copies[2].wait_recv()
            return near, self.from_leaves[1] + self.from_leaves[2]

    def gram_rings(ref, sems):
        return [
            Ring(
                lambda zz, cc, k=k: ref.at[k, zz, cc], ref.at[k, chip, core], (4 - k, 3 + k),
                sems[0].at[k], sems[1].at[k], sems[2].at[k], sems[3].at[k],
            )
            for k in (0, 1)
        ]

    pair_total, quad_total = Total(pair_parts, pair_bufs), Total(quad_parts, quad_bufs)
    pair_rings, quad_rings = gram_rings(grams_ref, gram_sems), gram_rings(quad_ref, last_sems)
    residual_b = residual8.astype(BF16)
    inner = ((0,), (0,))
    line = lax.broadcasted_iota(jnp.int32, (8, HALF), 0)

    def lines_of(k):
        rhs = dot(residual_b, upper[:, RANK * k : RANK * (k + 1)])
        rhs = rhs + dot(residual_b, lower[:, RANK * k : RANK * (k + 1)])
        return jnp.where(line == 0, rhs[:, 0:HALF], jnp.where(line == 1, rhs[:, HALF:], 0.0))

    def residue(offset, fresh=False):
        at = on(offset)
        block = cov[:, pl.ds(pl.multiple_of(at * 2 * rows, 128), 2 * rows)]
        term = dot(all_res[at].astype(BF16), block, ((1,), (1,)))
        residue_ref[...] = term if fresh else residue_ref[...] + term

    res_ring = Ring(
        lambda zz, cc: all_res.at[zz], all_res.at[chip], (4, 3), res_send, res_recv, None, None
    )
    for step in range(1, 5):
        serve(panel_rings[0], step)
        serve(panel_rings[1], step)
        if step == 1:
            res_copy.wait_recv()
            all_res[chip] = own_res[0] + own_res[1]
            res_ring.start()
        else:
            serve([res_ring], step - 1)
        absorb(0, step - 1)
        absorb(1, step - 1)
        residue(1 - step, step == 1)
        if step > 1:
            residue(step - 1)
    absorb(0, 4)
    absorb(1, 4)

    own_one = panels[0, chip, own_rows]
    own_two = panels[1, chip, own_rows]
    upper, lower = split(solved_ref[...])
    gram = dot(own_one, jnp.concatenate([upper, lower], axis=1), inner)
    gram = gram[:, 0:512] + gram[:, 512:1024]
    pair_parts[0] = gram[0:128]
    pair_parts[1, :, 0:384] = gram[128:256, 128:512]
    pair_parts[1, :, 384:512] = jnp.zeros((HALF, HALF), F32)
    pair_parts[1, 0:8, 384:512] = lines_of(0)
    pair_total.swap()
    gram = dot(own_two, jnp.concatenate([upper[:, 256:512], lower[:, 256:512]], axis=1), inner)
    gram = gram[:, 0:256] + gram[:, 256:512]
    quad_parts[0, :, 0:128] = gram[0:128, 128:256]
    quad_parts[0, :, 128:256] = jnp.zeros((HALF, HALF), F32)
    quad_parts[0, 0:8, 128:256] = lines_of(1)
    quad_parts[1, :, 0:128] = gram[0:128, 0:128]
    quad_parts[1, :, 128:256] = gram[128:256, 128:256]
    quad_total.swap()
    pair_total.spread()
    quad_total.spread()
    serve([res_ring], 4)
    residue(4)
    pair_total.cross()
    quad_total.cross()
    grams_ref[0, chip, core], grams_ref[1, chip, core] = pair_total.finish()
    for ring in pair_rings:
        ring.start()
    near, far = quad_total.finish()
    total = near + far
    quad_ref[0, chip, core] = total[:, 0:128]
    quad_ref[1, chip, core] = total[:, 128:256]
    for ring in quad_rings:
        ring.start()
    for step in range(1, 5):
        serve(pair_rings, step)
        serve(quad_rings, step)
    for step in range(0, 5):
        handed(pair_rings, step)
        handed(quad_rings, step)
    for copy in sent:
        copy.wait_send()


def inverse_of(value):
    guess = pl.reciprocal(value, approx=True)
    guess = guess * (2.0 - value * guess)
    return guess * (2.0 - value * guess)


def root_inverse(value):
    guess = lax.rsqrt(value)
    return guess * (1.5 - 0.5 * value * guess * guess)


def factor(matrices):
    count = len(matrices)
    tile = (count, 8, HALF)
    left = jnp.stack(matrices).reshape(count, 16, 8, HALF)
    lane = lax.broadcasted_iota(jnp.int32, tile, 2)
    line = lax.broadcasted_iota(jnp.int32, tile, 1)
    done = []
    for group in range(16):
        start = 8 * group
        top, left = left[:, 0], left[:, 1:]
        inside = (lane >= start) & (lane < start + 8)
        rows = [jnp.broadcast_to(top[:, j : j + 1], tile) for j in range(8)]
        p = {
            (i, j): jnp.broadcast_to(rows[i][:, :, start + j : start + j + 1], tile)
            for i in range(8)
            for j in range(i, 8)
        }
        rows = [
            jnp.where(inside, jnp.where(lane == start + j, 1.0, 0.0), rows[j]) for j in range(8)
        ]
        ties, scaled, final = [], [None] * 8, [None] * 8
        for i in range(0, 8, 2):
            a, b, d = p[i, i], p[i, i + 1], p[i + 1, i + 1]
            scale = inverse_of(a * d - b * b)
            i00, i01, i11 = d * scale, -b * scale, a * scale
            tie = {}
            for j in range(i + 2, 8):
                tie[j] = (
                    i00 * p[i, j] + i01 * p[i + 1, j],
                    i01 * p[i, j] + i11 * p[i + 1, j],
                )
            for m in range(i + 2, 8):
                for j in range(m, 8):
                    p[m, j] = p[m, j] - (p[i, m] * tie[j][0] + p[i + 1, m] * tie[j][1])
            for j in range(i + 2, 8):
                rows[j] = rows[j] - (tie[j][0] * rows[i] + tie[j][1] * rows[i + 1])
            scaled[i] = i00 * rows[i] + i01 * rows[i + 1]
            scaled[i + 1] = i01 * rows[i] + i11 * rows[i + 1]
            ties.append(tie)
            unit = root_inverse(a)
            final[i] = rows[i] * unit
            b = b * unit
            final[i + 1] = (rows[i + 1] - b * final[i]) * root_inverse(d - b * b)
        for i in (4, 2, 0):
            for j in range(7, i + 1, -1):
                scaled[i] = scaled[i] - ties[i // 2][j][0] * scaled[j]
                scaled[i + 1] = scaled[i + 1] - ties[i // 2][j][1] * scaled[j]
        whole = final[0]
        for j in range(1, 8):
            whole = jnp.where(line == j, final[j], whole)
        done.append(jnp.where(lane < start + 8, whole, 0.0))
        if group < 15:
            shape = left.shape
            columns = [
                jnp.broadcast_to(left[:, :, :, start + j : start + j + 1], shape)
                for j in range(8)
            ]
            left = jnp.where(inside[:, None], 0.0, left)
            for j in (6, 4, 2, 0):
                left = left - (
                    columns[j] * scaled[j][:, None] + columns[j + 1] * scaled[j + 1][:, None]
                )
    whole = jnp.stack(done, axis=1).reshape(count, HALF, HALF)
    return [whole[k] for k in range(count)]


def symmetric(block):
    return 0.5 * (block + block.T)


def solve_kernel(grams_ref, quad_ref, solved_ref, residue_ref, alpha_ref):
    line = lax.broadcasted_iota(jnp.int32, (HALF, HALF), 0)
    lane = lax.broadcasted_iota(jnp.int32, (HALF, HALF), 1)
    eye = jnp.where(line == lane, jnp.float32(1.0), 0.0)
    inner, outer = ((0,), (0,)), ((1,), (1,))

    def block(k, core, start, stop):
        return grams_ref[k, :, core, :, start:stop].reshape(HALF, stop - start)

    def quad_block(k, core):
        return quad_ref[k, :, core].reshape(HALF, HALF)

    def halves(packed):
        return [jnp.broadcast_to(packed[k : k + 1], (8, HALF)) for k in (0, 1)]

    rhs = [grams_ref[k, 0, 1, 0:8, 384:512] for k in (0, 1)]
    head = factor([eye + symmetric(block(k, 0, 0, 128)) for k in (0, 1)])
    tie = [mid(head[k], block(k, 0, 128, 256)) for k in (0, 1)]
    tail = factor(
        [eye + symmetric(block(k, 1, 0, 128)) - mid(tie[k], tie[k], inner) for k in (0, 1)]
    )

    cross, answers = [], []
    for k in (0, 1):
        upper = mid(head[k], block(k, 0, 256, 512))
        lower = mid(tail[k], block(k, 1, 128, 384) - mid(tie[k], upper, inner))
        cross += [upper, lower]
        f0, f1 = halves(rhs[k])
        y0 = mid(f0, head[k], outer)
        answers += [y0, mid(f1 - mid(y0, tie[k]), tail[k], outer)]
    near_cross = jnp.concatenate(cross[0:2], axis=0)
    near_answers = jnp.concatenate(answers[0:2], axis=1)
    cross = jnp.concatenate(cross, axis=0)
    answers = jnp.concatenate(answers, axis=1)
    gram = mid(cross, cross, inner)
    rest = jnp.concatenate(halves(quad_ref[1, 0, 0, 0:8]), axis=1) - mid(answers, cross)

    (quad_head,) = factor([eye + symmetric(quad_block(0, 1)) - gram[0:128, 0:128]])
    quad_tie = mid(quad_head, quad_block(0, 0) - gram[0:128, 128:256])
    (quad_tail,) = factor(
        [
            eye + symmetric(quad_block(1, 1)) - gram[128:256, 128:256]
            - mid(quad_tie, quad_tie, inner)
        ]
    )
    y0 = mid(rest[:, 0:128], quad_head, outer)
    y1 = mid(rest[:, 128:256] - mid(y0, quad_tie), quad_tail, outer)

    def back(y0, y1, first, between, last):
        x1 = mid(y1, last)
        return [mid(y0 - mid(x1, between, outer), first), x1]

    gain = back(y0, y1, quad_head, quad_tie, quad_tail)
    y = near_answers - mid(jnp.concatenate(gain, axis=1), near_cross, outer)
    shift = back(y[:, 0:128], y[:, 128:256], head[0], tie[0], tail[0])
    both = jnp.concatenate(shift + gain, axis=1)
    alpha = residue_ref[...] - mid(both, solved_ref[...], outer)
    alpha_ref[...] = alpha[0]


def per_device(inverse_cov, panel_one, panel_two, response, inputs, coeffs, degrees):
    codes, picks = degree_tables()
    rows = panel_one.shape[0]
    vmem = pl.BlockSpec(memory_space=pltpu.VMEM)
    hbm = pl.BlockSpec(memory_space=pltpu.HBM)
    dma = pltpu.SemaphoreType.DMA

    def sum_buffers(wide):
        return (
            pltpu.VMEM((HALF, wide), F32),
            pltpu.VMEM((CHIPS, 16, wide), F32),
            pltpu.VMEM((CHIPS - 1, 16, wide), F32),
            pltpu.VMEM((16, wide), F32),
            pltpu.VMEM((3, 16, wide), F32),
            dma((2,)), dma((2, CHIPS - 1)), dma((2, 3)),
        )

    ring_sems = (dma((2, 2, 4)), dma((2, 2, 4)), dma((2, 9)), dma((2, 9)))
    grams, quads, solved, residue = pl.pallas_call(
        gather_kernel,
        out_shape=(
            jax.ShapeDtypeStruct((2, CHIPS, 2, 16, 512), F32),
            jax.ShapeDtypeStruct((2, CHIPS, 2, 16, 128), F32),
            jax.ShapeDtypeStruct((rows, 2 * RANK), F32),
            jax.ShapeDtypeStruct((8, rows), F32),
        ),
        in_specs=[hbm] * 9,
        out_specs=(vmem,) * 4,
        scratch_shapes=[
            pltpu.VMEM(response.shape, F32),
            pltpu.VMEM(inputs.shape, F32),
            pltpu.VMEM(coeffs.shape, F32),
            pltpu.VMEM(degrees.shape, jnp.int32),
            pltpu.VMEM(codes.shape, jnp.int32),
            pltpu.VMEM(picks.shape, BF16),
            pltpu.VMEM(inverse_cov.shape, BF16),
            pltpu.VMEM((2, CHIPS, 2 * rows, RANK), BF16),
            pltpu.VMEM((8, rows), F32),
            pltpu.VMEM((2, 8, 2 * rows), F32),
            pltpu.VMEM((CHIPS, 8, 2 * rows), F32),
            pltpu.VMEM((2, HALF, 512), F32),
            pltpu.VMEM((2, HALF, 256), F32),
            dma((9,)),
            dma((4, 2, 4)), dma((4, 2, 4)),
            dma((4, 9)), dma((4, 9)),
            dma((2, 4)), dma((2, 4)),
            dma, dma,
            sum_buffers(512), sum_buffers(256),
            ring_sems, ring_sems,
        ],
        compiler_params=pltpu.CompilerParams(
            collective_id=0, has_side_effects=True, vmem_limit_bytes=63 * 1024 * 1024
        ),
    )(
        inverse_cov, panel_one, panel_two, response, inputs, coeffs, degrees,
        jnp.asarray(codes), jnp.asarray(picks),
    )
    alpha = pl.pallas_call(
        solve_kernel,
        out_shape=jax.ShapeDtypeStruct((rows,), F32),
        in_specs=[vmem] * 4,
        out_specs=vmem,
        compiler_params=pltpu.CompilerParams(vmem_limit_bytes=63 * 1024 * 1024),
    )(grams, quads, solved, residue)
    return alpha


def solution(mesh):
    in_specs = (
        P(("runs", "rank"), None),
        P(("runs", "rank"), None),
        P(("runs", "rank"), None),
        P(("runs", "rank")),
        P(None, ("runs", "rank")),
        P(),
        P(),
    )
    out_specs = P(("runs", "rank"))
    return jax.shard_map(
        per_device, mesh=mesh, in_specs=in_specs, out_specs=out_specs, check_vma=False
    )
```

```python
import math

import jax
import jax.numpy as jnp
import numpy as np
from jax import lax
from jax.experimental import pallas as pl
from jax.experimental.pallas import tpu as pltpu
from jax.sharding import PartitionSpec as P

MESH = pl.DeviceIdType.MESH
F32 = jnp.float32
BF16 = jnp.bfloat16
HIGHEST = lax.Precision.HIGHEST
RANK = 256
HALF = 128
CHIPS = 8


def degree_tables():
    triples = [
        (a, b, c) for a in range(8) for b in range(8) for c in range(8) if a + b + c <= 7
    ]
    codes = np.full((HALF, 1), -1, np.int32)
    picks = np.zeros((6, HALF, 64), np.float32)
    for row, triple in enumerate(triples):
        codes[row, 0] = triple[0] + 8 * triple[1] + 64 * triple[2]
        for column in range(6):
            picks[column, row, triple[column % 3] * 8 + column] = 1.0
    return codes, np.tile(picks.reshape(6 * HALF, 64), (1, 3)).astype(jnp.bfloat16)


def dot(left, right, dims=((1,), (0,)), precision=None):
    return lax.dot_general(
        left, right, (dims, ((), ())), precision=precision, preferred_element_type=F32
    )


def high(left, right, dims=((1,), (0,))):
    return dot(left, right, dims, HIGHEST)


def pieces(value):
    parts = []
    for _ in range(3):
        parts.append(value.astype(BF16))
        value = value - parts[-1].astype(F32)
    return parts


def split(value):
    upper = value.astype(BF16)
    return upper, (value - upper.astype(F32)).astype(BF16)


def mid(left, right, dims=((1,), (0,))):
    upper, lower = split(right)
    if dims[0] == (0,):
        first, second = split(left)
        return dot(first, upper, dims) + dot(second, upper, dims) + dot(first, lower, dims)
    count = left.shape[0]
    first = left.astype(BF16)
    whole = first.astype(F32)
    both = dot(jnp.concatenate([whole, left - whole], axis=0).astype(BF16), upper, dims)
    return both[:count] + both[count:] + dot(first, lower, dims)


def gather_kernel(
    cov_ref, one_ref, two_ref, response_hbm, inputs_hbm, coeffs_hbm, degrees_hbm, codes_hbm,
    picks_hbm, alpha_ref, grams_ref, quad_ref, solved_ref, residue_ref,
    response_ref, inputs_ref, coeffs_ref, degrees_ref, codes_ref, picks_ref, cov, panels,
    points, own_res, all_res, pair_parts, quad_parts, local_sem, panel_send, panel_recv, core_send,
    core_recv, res_send, res_recv, pick_send, pick_recv, pair_bufs, quad_bufs, gram_sems, last_sems,
):
    leaf = lax.axis_index("runs")
    place = lax.axis_index("rank")
    chip, core = place // 2, place % 2
    rows = one_ref.shape[0]
    own_rows = pl.ds(pl.multiple_of(core * rows, 64), rows)

    def on(offset):
        return lax.rem(chip + offset + CHIPS, CHIPS)

    def chip_at(offset):
        return (leaf, 2 * on(offset) + core)

    sibling = (leaf, 2 * chip + 1 - core)

    def leaf_at(bits):
        return (leaf ^ bits, place)

    peers = [chip_at(o) for o in range(1, CHIPS)] + [sibling] + [leaf_at(b) for b in (1, 2, 3)]
    barrier = pltpu.get_barrier_semaphore()
    for peer in peers:
        pl.semaphore_signal(barrier, inc=1, device_id=peer, device_id_type=MESH)

    operands = (one_ref, two_ref)
    local = [
        pltpu.make_async_copy(one_ref, panels.at[0, chip, own_rows], local_sem.at[0]),
        pltpu.make_async_copy(two_ref, panels.at[1, chip, own_rows], local_sem.at[1]),
        pltpu.make_async_copy(cov_ref, cov, local_sem.at[2]),
    ]
    small = [
        pltpu.make_async_copy(src, dst, local_sem.at[3 + k])
        for k, (src, dst) in enumerate(
            [
                (response_hbm, response_ref), (inputs_hbm, inputs_ref), (coeffs_hbm, coeffs_ref),
                (degrees_hbm, degrees_ref), (codes_hbm, codes_ref), (picks_hbm, picks_ref),
            ]
        )
    ]
    for copy in small:
        copy.start()
    for copy in local:
        copy.start()
    pl.semaphore_wait(barrier, len(peers))

    sent = []

    def push(src, dst, send, recv, device):
        copy = pltpu.make_async_remote_copy(
            src_ref=src, dst_ref=dst, send_sem=send, recv_sem=recv, device_id=device,
            device_id_type=MESH,
        )
        copy.start()
        sent.append(copy)
        return copy

    class Ring:
        def __init__(self, view, own, steps, send, recv, core_sends, core_recvs):
            self.view, self.own, self.steps = view, own, steps
            self.send, self.recv = send, recv
            self.core_sends, self.core_recvs = core_sends, core_recvs
            self.flying, self.handed = {}, {}

        def forward(self, way, step, src):
            offset = -(step - 1) if way == 0 else step - 1
            self.flying[way, step] = push(
                src, self.view(on(offset), core), self.send.at[way, step - 1],
                self.recv.at[way, step - 1], chip_at(1 if way == 0 else -1),
            )

        def hand(self, way, step, src):
            offset = -step if way == 0 else step
            slot = 4 * way + step
            self.handed[way, step] = push(
                src, self.view(on(offset), core), self.core_sends.at[slot],
                self.core_recvs.at[slot], sibling,
            )

        def start(self):
            for way in (0, 1):
                self.forward(way, 1, self.own)
            if self.core_sends is not None:
                self.hand(0, 0, self.own)

        def arrive(self, way, step):
            if step > self.steps[way]:
                return
            self.flying[way, step].wait_recv()
            block = self.view(on(-step if way == 0 else step), core)
            if step < self.steps[way]:
                self.forward(way, step + 1, block)
            if self.core_sends is not None:
                self.hand(way, step, block)

        def handed_over(self, way, step):
            if (way, step) in self.handed:
                self.handed[way, step].wait_recv()

    half = rows // 2

    def panel_view(k, h):
        return lambda zz, cc: panels.at[k, zz, pl.ds(pl.multiple_of(cc * rows + h * half, 32), half)]

    panel_rings = [
        [
            Ring(
                panel_view(k, h), operands[k].at[pl.ds(h * half, half)], (4 - h, 3 + h),
                panel_send.at[2 * k + h], panel_recv.at[2 * k + h], core_send.at[2 * k + h],
                core_recv.at[2 * k + h],
            )
            for h in (0, 1)
        ]
        for k in (0, 1)
    ]
    for ring in panel_rings[0] + panel_rings[1]:
        ring.start()

    for copy in small:
        copy.wait()
    points[...] = jnp.zeros(points.shape, F32)
    points[0:6, :] = inputs_ref[...]
    x = points[...]
    levels = [jnp.ones_like(x), x]
    for k in range(1, 7):
        levels.append(((2 * k + 1) * x * levels[k] - k * levels[k - 1]) / (k + 1))
    levels = [math.sqrt(2 * k + 1) * level for k, level in enumerate(levels)]
    factors = dot(picks_ref[...], jnp.concatenate(pieces(jnp.concatenate(levels, axis=0)), axis=0))
    first = factors[0:128] * factors[128:256] * factors[256:384]
    second = factors[384:512] * factors[512:640] * factors[640:768]
    orders = degrees_ref[...]
    left_code = orders[0:1] + 8 * orders[1:2] + 64 * orders[2:3]
    right_code = orders[3:4] + 8 * orders[4:5] + 64 * orders[5:6]
    left = jnp.where(codes_ref[...] == left_code, coeffs_ref[...].reshape(1, -1), 0.0)
    right = jnp.where(codes_ref[...] == right_code, 1.0, 0.0).astype(BF16)
    table = dot(jnp.concatenate(pieces(left), axis=0), right, ((1,), (1,)))
    table = table[0:128] + table[128:256] + table[256:384]
    trend = jnp.sum(high(table, first, ((0,), (0,))) * second, axis=0, keepdims=True)
    residual = (response_ref[...].reshape(1, rows) - trend).astype(BF16).astype(F32)
    residual8 = jnp.broadcast_to(residual, (8, rows))
    own_res[0] = jnp.zeros((8, 2 * rows), F32)

    @pl.when(core == 0)
    def _():
        own_res[0, :, 0:rows] = residual8

    @pl.when(core == 1)
    def _():
        own_res[0, :, rows : 2 * rows] = residual8

    res_copy = push(own_res.at[0], own_res.at[1], pick_send, pick_recv, sibling)
    for copy in local:
        copy.wait()

    def apply(k, offset, fresh=False):
        at = on(offset)
        block = cov[:, pl.ds(pl.multiple_of(at * 2 * rows, 128), 2 * rows)]
        term = dot(block, panels[k, at])
        lanes = slice(RANK * k, RANK * (k + 1))
        solved_ref[:, lanes] = term if fresh else solved_ref[:, lanes] + term

    def serve(rings, step):
        for ring in rings:
            ring.arrive(0, step)
            ring.arrive(1, step)

    def handed(rings, step):
        for ring in rings:
            ring.handed_over(0, step)
            ring.handed_over(1, step)

    def absorb(k, step):
        handed(panel_rings[k], step)
        apply(k, step, step == 0)
        if 0 < step < 4:
            apply(k, -step)

    class Total:
        def __init__(self, parts, bufs):
            self.parts = parts
            (self.from_core, self.mine, self.from_chips, self.leaf_sum, self.from_leaves) = bufs[0:5]
            (self.sum_sem, self.chip_sem, self.leaf_sem) = bufs[5:8]

        def swap(self):
            self.swapped = push(
                self.parts.at[1 - core], self.from_core, self.sum_sem.at[0], self.sum_sem.at[1],
                sibling,
            )

        def spread(self):
            self.swapped.wait_recv()
            for k in range(CHIPS):
                band = slice(16 * k, 16 * (k + 1))
                self.mine[k] = self.parts[core, band] + self.from_core[band]
            self.copies = [
                push(
                    self.mine.at[on(o)], self.from_chips.at[o - 1], self.chip_sem.at[0, o - 1],
                    self.chip_sem.at[1, o - 1], chip_at(o),
                )
                for o in range(1, CHIPS)
            ]

        def cross(self):
            self.total = self.mine[chip]
            for o in range(1, CHIPS):
                self.copies[o - 1].wait_recv()
                self.total = self.total + self.from_chips[o - 1]
            self.leaf_sum[...] = self.total
            self.copies = [
                push(
                    self.leaf_sum, self.from_leaves.at[b - 1], self.leaf_sem.at[0, b - 1],
                    self.leaf_sem.at[1, b - 1], leaf_at(b),
                )
                for b in (1, 2, 3)
            ]

        def finish(self):
            self.copies[0].wait_recv()
            near = self.leaf_sum[...] + self.from_leaves[0]
            self.copies[1].wait_recv()
            self.copies[2].wait_recv()
            return near, self.from_leaves[1] + self.from_leaves[2]

    def gram_rings(ref, sems):
        return [
            Ring(
                lambda zz, cc, k=k: ref.at[k, zz, cc], ref.at[k, chip, core], (4 - k, 3 + k),
                sems[0].at[k], sems[1].at[k], sems[2].at[k], sems[3].at[k],
            )
            for k in (0, 1)
        ]

    pair_total, quad_total = Total(pair_parts, pair_bufs), Total(quad_parts, quad_bufs)
    pair_rings, quad_rings = gram_rings(grams_ref, gram_sems), gram_rings(quad_ref, last_sems)
    residual_b = residual8.astype(BF16)
    inner = ((0,), (0,))
    line = lax.broadcasted_iota(jnp.int32, (8, HALF), 0)

    def lines_of(k):
        rhs = dot(residual_b, upper[:, RANK * k : RANK * (k + 1)])
        rhs = rhs + dot(residual_b, lower[:, RANK * k : RANK * (k + 1)])
        return jnp.where(line == 0, rhs[:, 0:HALF], jnp.where(line == 1, rhs[:, HALF:], 0.0))

    def residue(offset, fresh=False):
        at = on(offset)
        block = cov[:, pl.ds(pl.multiple_of(at * 2 * rows, 128), 2 * rows)]
        term = dot(all_res[at].astype(BF16), block, ((1,), (1,)))
        residue_ref[...] = term if fresh else residue_ref[...] + term

    res_ring = Ring(
        lambda zz, cc: all_res.at[zz], all_res.at[chip], (4, 3), res_send, res_recv, None, None
    )
    for step in range(1, 5):
        serve(panel_rings[0], step)
        serve(panel_rings[1], step)
        if step == 1:
            res_copy.wait_recv()
            all_res[chip] = own_res[0] + own_res[1]
            res_ring.start()
        else:
            serve([res_ring], step - 1)
        absorb(0, step - 1)
        absorb(1, step - 1)
        residue(1 - step, step == 1)
        if step > 1:
            residue(step - 1)
    absorb(0, 4)
    absorb(1, 4)

    own_one = panels[0, chip, own_rows]
    own_two = panels[1, chip, own_rows]
    upper, lower = split(solved_ref[...])
    gram = dot(own_one, jnp.concatenate([upper, lower], axis=1), inner)
    gram = gram[:, 0:512] + gram[:, 512:1024]
    pair_parts[0] = gram[0:128]
    pair_parts[1, :, 0:384] = gram[128:256, 128:512]
    pair_parts[1, :, 384:512] = jnp.zeros((HALF, HALF), F32)
    pair_parts[1, 0:8, 384:512] = lines_of(0)
    pair_total.swap()
    gram = dot(own_two, jnp.concatenate([upper[:, 256:512], lower[:, 256:512]], axis=1), inner)
    gram = gram[:, 0:256] + gram[:, 256:512]
    quad_parts[0, :, 0:128] = gram[0:128, 128:256]
    quad_parts[0, :, 128:256] = jnp.zeros((HALF, HALF), F32)
    quad_parts[0, 0:8, 128:256] = lines_of(1)
    quad_parts[1, :, 0:128] = gram[0:128, 0:128]
    quad_parts[1, :, 128:256] = gram[128:256, 128:256]
    quad_total.swap()
    pair_total.spread()
    quad_total.spread()
    serve([res_ring], 4)
    residue(4)
    pair_total.cross()
    quad_total.cross()
    grams_ref[0, chip, core], grams_ref[1, chip, core] = pair_total.finish()
    for ring in pair_rings:
        ring.start()
    near, far = quad_total.finish()
    total = near + far
    quad_ref[0, chip, core] = total[:, 0:128]
    quad_ref[1, chip, core] = total[:, 128:256]
    for ring in quad_rings:
        ring.start()
    for step in range(1, 5):
        serve(pair_rings, step)
        serve(quad_rings, step)
    for step in range(0, 5):
        handed(pair_rings, step)
        handed(quad_rings, step)
    solve(grams_ref, quad_ref, solved_ref, residue_ref, alpha_ref)
    for copy in sent:
        copy.wait_send()


def inverse_of(value):
    guess = pl.reciprocal(value, approx=True)
    guess = guess * (2.0 - value * guess)
    return guess * (2.0 - value * guess)


def root_inverse(value):
    guess = lax.rsqrt(value)
    return guess * (1.5 - 0.5 * value * guess * guess)


def factor(matrices):
    count = len(matrices)
    tile = (8, HALF)
    left = jnp.stack(matrices).reshape(count, 16, 8, HALF)
    lane = lax.broadcasted_iota(jnp.int32, tile, 1)
    line = lax.broadcasted_iota(jnp.int32, tile, 0)

    def join(pieces):
        wide = [jnp.broadcast_to(piece, tile) for piece in pieces]
        return wide[0] if count == 1 else jnp.where(line < 4, wide[0], wide[1])

    def part(value):
        if count == 1:
            return value[None]
        return jnp.stack([jnp.broadcast_to(value[4 * k : 4 * k + 1], tile) for k in (0, 1)])

    done = []
    for group in range(16):
        start = 8 * group
        top, left = left[:, 0], left[:, 1:]
        inside = (lane >= start) & (lane < start + 8)
        rows = [join([top[k, j : j + 1] for k in range(count)]) for j in range(8)]
        p = {
            (i, j): jnp.broadcast_to(rows[i][:, start + j : start + j + 1], tile)
            for i in range(8)
            for j in range(i, 8)
        }
        rows = [
            jnp.where(inside, jnp.where(lane == start + j, 1.0, 0.0), rows[j]) for j in range(8)
        ]
        ties, scaled, final = [], [None] * 8, [None] * 8
        for i in range(0, 8, 2):
            a, b, d = p[i, i], p[i, i + 1], p[i + 1, i + 1]
            scale = inverse_of(a * d - b * b)
            i00, i01, i11 = d * scale, -b * scale, a * scale
            tie = {}
            for j in range(i + 2, 8):
                tie[j] = (
                    i00 * p[i, j] + i01 * p[i + 1, j],
                    i01 * p[i, j] + i11 * p[i + 1, j],
                )
            for m in range(i + 2, 8):
                for j in range(m, 8):
                    p[m, j] = p[m, j] - (p[i, m] * tie[j][0] + p[i + 1, m] * tie[j][1])
            for j in range(i + 2, 8):
                rows[j] = rows[j] - (tie[j][0] * rows[i] + tie[j][1] * rows[i + 1])
            scaled[i] = i00 * rows[i] + i01 * rows[i + 1]
            scaled[i + 1] = i01 * rows[i] + i11 * rows[i + 1]
            ties.append(tie)
            unit = root_inverse(a)
            final[i] = rows[i] * unit
            b = b * unit
            final[i + 1] = (rows[i + 1] - b * final[i]) * root_inverse(d - b * b)
        for i in (4, 2, 0):
            for j in range(7, i + 1, -1):
                scaled[i] = scaled[i] - ties[i // 2][j][0] * scaled[j]
                scaled[i + 1] = scaled[i + 1] - ties[i // 2][j][1] * scaled[j]
        whole = part(final[0])
        for j in range(1, 8):
            whole = jnp.where(line == j, part(final[j]), whole)
        scaled = [part(value)[:, None] for value in scaled]
        done.append(jnp.where(lane < start + 8, whole, 0.0))
        if group < 15:
            shape = left.shape
            columns = [
                jnp.broadcast_to(left[:, :, :, start + j : start + j + 1], shape)
                for j in range(8)
            ]
            left = jnp.where(inside, 0.0, left)
            for j in (6, 4, 2, 0):
                left = left - (
                    columns[j] * scaled[j] + columns[j + 1] * scaled[j + 1]
                )
    whole = jnp.stack(done, axis=1).reshape(count, HALF, HALF)
    return [whole[k] for k in range(count)]


def symmetric(block):
    return 0.5 * (block + block.T)


def solve(grams_ref, quad_ref, solved_ref, residue_ref, alpha_ref):
    line = lax.broadcasted_iota(jnp.int32, (HALF, HALF), 0)
    lane = lax.broadcasted_iota(jnp.int32, (HALF, HALF), 1)
    eye = jnp.where(line == lane, jnp.float32(1.0), 0.0)
    inner, outer = ((0,), (0,)), ((1,), (1,))

    def block(k, core, start, stop):
        return grams_ref[k, :, core, :, start:stop].reshape(HALF, stop - start)

    def quad_block(k, core):
        return quad_ref[k, :, core].reshape(HALF, HALF)

    def halves(packed):
        return [jnp.broadcast_to(packed[k : k + 1], (8, HALF)) for k in (0, 1)]

    rhs = [grams_ref[k, 0, 1, 0:8, 384:512] for k in (0, 1)]
    head = factor([eye + symmetric(block(k, 0, 0, 128)) for k in (0, 1)])
    tie = [mid(head[k], block(k, 0, 128, 256)) for k in (0, 1)]
    tail = factor(
        [eye + symmetric(block(k, 1, 0, 128)) - mid(tie[k], tie[k], inner) for k in (0, 1)]
    )

    cross, answers = [], []
    for k in (0, 1):
        upper = mid(head[k], block(k, 0, 256, 512))
        lower = mid(tail[k], block(k, 1, 128, 384) - mid(tie[k], upper, inner))
        cross += [upper, lower]
        f0, f1 = halves(rhs[k])
        y0 = mid(f0, head[k], outer)
        answers += [y0, mid(f1 - mid(y0, tie[k]), tail[k], outer)]
    near_cross = jnp.concatenate(cross[0:2], axis=0)
    near_answers = jnp.concatenate(answers[0:2], axis=1)
    cross = jnp.concatenate(cross, axis=0)
    answers = jnp.concatenate(answers, axis=1)
    gram = mid(cross, cross, inner)
    rest = jnp.concatenate(halves(quad_ref[1, 0, 0, 0:8]), axis=1) - mid(answers, cross)

    (quad_head,) = factor([eye + symmetric(quad_block(0, 1)) - gram[0:128, 0:128]])
    quad_tie = mid(quad_head, quad_block(0, 0) - gram[0:128, 128:256])
    (quad_tail,) = factor(
        [
            eye + symmetric(quad_block(1, 1)) - gram[128:256, 128:256]
            - mid(quad_tie, quad_tie, inner)
        ]
    )
    y0 = mid(rest[:, 0:128], quad_head, outer)
    y1 = mid(rest[:, 128:256] - mid(y0, quad_tie), quad_tail, outer)

    def back(y0, y1, first, between, last):
        x1 = mid(y1, last)
        return [mid(y0 - mid(x1, between, outer), first), x1]

    gain = back(y0, y1, quad_head, quad_tie, quad_tail)
    y = near_answers - mid(jnp.concatenate(gain, axis=1), near_cross, outer)
    shift = back(y[:, 0:128], y[:, 128:256], head[0], tie[0], tail[0])
    both = jnp.concatenate(shift + gain, axis=1)
    alpha = residue_ref[...] - mid(both, solved_ref[...], outer)
    alpha_ref[...] = alpha[0]


def per_device(inverse_cov, panel_one, panel_two, response, inputs, coeffs, degrees):
    codes, picks = degree_tables()
    rows = panel_one.shape[0]
    vmem = pl.BlockSpec(memory_space=pltpu.VMEM)
    hbm = pl.BlockSpec(memory_space=pltpu.HBM)
    dma = pltpu.SemaphoreType.DMA

    def sum_buffers(wide):
        return (
            pltpu.VMEM((HALF, wide), F32),
            pltpu.VMEM((CHIPS, 16, wide), F32),
            pltpu.VMEM((CHIPS - 1, 16, wide), F32),
            pltpu.VMEM((16, wide), F32),
            pltpu.VMEM((3, 16, wide), F32),
            dma((2,)), dma((2, CHIPS - 1)), dma((2, 3)),
        )

    ring_sems = (dma((2, 2, 4)), dma((2, 2, 4)), dma((2, 9)), dma((2, 9)))
    return pl.pallas_call(
        gather_kernel,
        out_shape=jax.ShapeDtypeStruct((rows,), F32),
        in_specs=[hbm] * 9,
        out_specs=vmem,
        scratch_shapes=[
            pltpu.VMEM((2, CHIPS, 2, 16, 512), F32),
            pltpu.VMEM((2, CHIPS, 2, 16, 128), F32),
            pltpu.VMEM((rows, 2 * RANK), F32),
            pltpu.VMEM((8, rows), F32),
            pltpu.VMEM(response.shape, F32),
            pltpu.VMEM(inputs.shape, F32),
            pltpu.VMEM(coeffs.shape, F32),
            pltpu.VMEM(degrees.shape, jnp.int32),
            pltpu.VMEM(codes.shape, jnp.int32),
            pltpu.VMEM(picks.shape, BF16),
            pltpu.VMEM(inverse_cov.shape, BF16),
            pltpu.VMEM((2, CHIPS, 2 * rows, RANK), BF16),
            pltpu.VMEM((8, rows), F32),
            pltpu.VMEM((2, 8, 2 * rows), F32),
            pltpu.VMEM((CHIPS, 8, 2 * rows), F32),
            pltpu.VMEM((2, HALF, 512), F32),
            pltpu.VMEM((2, HALF, 256), F32),
            dma((9,)),
            dma((4, 2, 4)), dma((4, 2, 4)),
            dma((4, 9)), dma((4, 9)),
            dma((2, 4)), dma((2, 4)),
            dma, dma,
            sum_buffers(512), sum_buffers(256),
            ring_sems, ring_sems,
        ],
        compiler_params=pltpu.CompilerParams(
            collective_id=0, has_side_effects=True, vmem_limit_bytes=63 * 1024 * 1024
        ),
    )(
        inverse_cov, panel_one, panel_two, response, inputs, coeffs, degrees,
        jnp.asarray(codes), jnp.asarray(picks),
    )


def solution(mesh):
    in_specs = (
        P(("runs", "rank"), None),
        P(("runs", "rank"), None),
        P(("runs", "rank"), None),
        P(("runs", "rank")),
        P(None, ("runs", "rank")),
        P(),
        P(),
    )
    out_specs = P(("runs", "rank"))
    return jax.shard_map(
        per_device, mesh=mesh, in_specs=in_specs, out_specs=out_specs, check_vma=False
    )
```

```python
import math

import jax
import jax.numpy as jnp
import numpy as np
from jax import lax
from jax.experimental import pallas as pl
from jax.experimental.pallas import tpu as pltpu
from jax.sharding import PartitionSpec as P

MESH = pl.DeviceIdType.MESH
F32 = jnp.float32
BF16 = jnp.bfloat16
HIGHEST = lax.Precision.HIGHEST
RANK = 256
HALF = 128
CHIPS = 8


def degree_tables():
    triples = [
        (a, b, c) for a in range(8) for b in range(8) for c in range(8) if a + b + c <= 7
    ]
    codes = np.full((HALF, 1), -1, np.int32)
    picks = np.zeros((6, HALF, 64), np.float32)
    for row, triple in enumerate(triples):
        codes[row, 0] = triple[0] + 8 * triple[1] + 64 * triple[2]
        for column in range(6):
            picks[column, row, triple[column % 3] * 8 + column] = 1.0
    return codes, np.tile(picks.reshape(6 * HALF, 64), (1, 3)).astype(jnp.bfloat16)


def dot(left, right, dims=((1,), (0,)), precision=None):
    return lax.dot_general(
        left, right, (dims, ((), ())), precision=precision, preferred_element_type=F32
    )


def high(left, right, dims=((1,), (0,))):
    return dot(left, right, dims, HIGHEST)


def pieces(value):
    parts = []
    for _ in range(3):
        parts.append(value.astype(BF16))
        value = value - parts[-1].astype(F32)
    return parts


def split(value):
    upper = value.astype(BF16)
    return upper, (value - upper.astype(F32)).astype(BF16)


def mid(left, right, dims=((1,), (0,))):
    upper, lower = split(right)
    if dims[0] == (0,):
        first, second = split(left)
        return dot(first, upper, dims) + dot(second, upper, dims) + dot(first, lower, dims)
    count = left.shape[0]
    first = left.astype(BF16)
    whole = first.astype(F32)
    both = dot(jnp.concatenate([whole, left - whole], axis=0).astype(BF16), upper, dims)
    return both[:count] + both[count:] + dot(first, lower, dims)


def gather_kernel(
    cov_ref, one_ref, two_ref, response_hbm, inputs_hbm, coeffs_hbm, degrees_hbm, codes_hbm,
    picks_hbm, alpha_ref, grams_ref, quad_ref, solved_ref, residue_ref,
    response_ref, inputs_ref, coeffs_ref, degrees_ref, codes_ref, picks_ref, cov, panels,
    points, own_res, all_res, pair_parts, quad_parts, local_sem, panel_send, panel_recv, core_send,
    core_recv, res_send, res_recv, pick_send, pick_recv, pair_bufs, quad_bufs, gram_sems, last_sems,
):
    leaf = lax.axis_index("runs")
    place = lax.axis_index("rank")
    chip, core = place // 2, place % 2
    rows = one_ref.shape[0]
    own_rows = pl.ds(pl.multiple_of(core * rows, 64), rows)

    def on(offset):
        return lax.rem(chip + offset + CHIPS, CHIPS)

    def chip_at(offset):
        return (leaf, 2 * on(offset) + core)

    sibling = (leaf, 2 * chip + 1 - core)

    def leaf_at(bits):
        return (leaf ^ bits, place)

    peers = [chip_at(o) for o in range(1, CHIPS)] + [sibling] + [leaf_at(b) for b in (1, 2, 3)]
    barrier = pltpu.get_barrier_semaphore()
    for peer in peers:
        pl.semaphore_signal(barrier, inc=1, device_id=peer, device_id_type=MESH)

    operands = (one_ref, two_ref)
    local = [
        pltpu.make_async_copy(one_ref, panels.at[0, chip, own_rows], local_sem.at[0]),
        pltpu.make_async_copy(two_ref, panels.at[1, chip, own_rows], local_sem.at[1]),
        pltpu.make_async_copy(cov_ref, cov, local_sem.at[2]),
    ]
    small = [
        pltpu.make_async_copy(src, dst, local_sem.at[3 + k])
        for k, (src, dst) in enumerate(
            [
                (response_hbm, response_ref), (inputs_hbm, inputs_ref), (coeffs_hbm, coeffs_ref),
                (degrees_hbm, degrees_ref), (codes_hbm, codes_ref), (picks_hbm, picks_ref),
            ]
        )
    ]
    for copy in small:
        copy.start()
    for copy in local:
        copy.start()
    pl.semaphore_wait(barrier, len(peers))

    sent = []

    def push(src, dst, send, recv, device):
        copy = pltpu.make_async_remote_copy(
            src_ref=src, dst_ref=dst, send_sem=send, recv_sem=recv, device_id=device,
            device_id_type=MESH,
        )
        copy.start()
        sent.append(copy)
        return copy

    class Ring:
        def __init__(self, view, own, steps, send, recv, core_sends, core_recvs):
            self.view, self.own, self.steps = view, own, steps
            self.send, self.recv = send, recv
            self.core_sends, self.core_recvs = core_sends, core_recvs
            self.flying, self.handed = {}, {}

        def forward(self, way, step, src):
            offset = -(step - 1) if way == 0 else step - 1
            self.flying[way, step] = push(
                src, self.view(on(offset), core), self.send.at[way, step - 1],
                self.recv.at[way, step - 1], chip_at(1 if way == 0 else -1),
            )

        def hand(self, way, step, src):
            offset = -step if way == 0 else step
            slot = 4 * way + step
            self.handed[way, step] = push(
                src, self.view(on(offset), core), self.core_sends.at[slot],
                self.core_recvs.at[slot], sibling,
            )

        def start(self):
            for way in (0, 1):
                self.forward(way, 1, self.own)
            if self.core_sends is not None:
                self.hand(0, 0, self.own)

        def arrive(self, way, step):
            if step > self.steps[way]:
                return
            self.flying[way, step].wait_recv()
            block = self.view(on(-step if way == 0 else step), core)
            if step < self.steps[way]:
                self.forward(way, step + 1, block)
            if self.core_sends is not None:
                self.hand(way, step, block)

        def handed_over(self, way, step):
            if (way, step) in self.handed:
                self.handed[way, step].wait_recv()

    half = rows // 2

    def panel_view(k, h):
        return lambda zz, cc: panels.at[k, zz, pl.ds(pl.multiple_of(cc * rows + h * half, 32), half)]

    panel_rings = [
        [
            Ring(
                panel_view(k, h), operands[k].at[pl.ds(h * half, half)], (4 - h, 3 + h),
                panel_send.at[2 * k + h], panel_recv.at[2 * k + h], core_send.at[2 * k + h],
                core_recv.at[2 * k + h],
            )
            for h in (0, 1)
        ]
        for k in (0, 1)
    ]
    for ring in panel_rings[0] + panel_rings[1]:
        ring.start()

    for copy in small:
        copy.wait()
    points[...] = jnp.zeros(points.shape, F32)
    points[0:6, :] = inputs_ref[...]
    x = points[...]
    levels = [jnp.ones_like(x), x]
    for k in range(1, 7):
        levels.append(((2 * k + 1) * x * levels[k] - k * levels[k - 1]) / (k + 1))
    levels = [math.sqrt(2 * k + 1) * level for k, level in enumerate(levels)]
    factors = dot(picks_ref[...], jnp.concatenate(pieces(jnp.concatenate(levels, axis=0)), axis=0))
    first = factors[0:128] * factors[128:256] * factors[256:384]
    second = factors[384:512] * factors[512:640] * factors[640:768]
    orders = degrees_ref[...]
    left_code = orders[0:1] + 8 * orders[1:2] + 64 * orders[2:3]
    right_code = orders[3:4] + 8 * orders[4:5] + 64 * orders[5:6]
    left = jnp.where(codes_ref[...] == left_code, coeffs_ref[...].reshape(1, -1), 0.0)
    right = jnp.where(codes_ref[...] == right_code, 1.0, 0.0).astype(BF16)
    table = dot(jnp.concatenate(pieces(left), axis=0), right, ((1,), (1,)))
    table = table[0:128] + table[128:256] + table[256:384]
    trend = jnp.sum(high(table, first, ((0,), (0,))) * second, axis=0, keepdims=True)
    residual = (response_ref[...].reshape(1, rows) - trend).astype(BF16).astype(F32)
    residual8 = jnp.broadcast_to(residual, (8, rows))
    own_res[0] = jnp.zeros((8, 2 * rows), F32)

    @pl.when(core == 0)
    def _():
        own_res[0, :, 0:rows] = residual8

    @pl.when(core == 1)
    def _():
        own_res[0, :, rows : 2 * rows] = residual8

    res_copy = push(own_res.at[0], own_res.at[1], pick_send, pick_recv, sibling)
    for copy in local:
        copy.wait()

    def apply(k, offset, fresh=False):
        at = on(offset)
        block = cov[:, pl.ds(pl.multiple_of(at * 2 * rows, 128), 2 * rows)]
        term = dot(block, panels[k, at])
        lanes = slice(RANK * k, RANK * (k + 1))
        solved_ref[:, lanes] = term if fresh else solved_ref[:, lanes] + term

    def serve(rings, step):
        for ring in rings:
            ring.arrive(0, step)
            ring.arrive(1, step)

    def handed(rings, step):
        for ring in rings:
            ring.handed_over(0, step)
            ring.handed_over(1, step)

    def absorb(k, step):
        handed(panel_rings[k], step)
        apply(k, step, step == 0)
        if 0 < step < 4:
            apply(k, -step)

    class Total:
        def __init__(self, parts, bufs):
            self.parts = parts
            (self.from_core, self.mine, self.from_chips, self.leaf_sum, self.from_leaves) = bufs[0:5]
            (self.sum_sem, self.chip_sem, self.leaf_sem) = bufs[5:8]

        def swap(self):
            self.swapped = push(
                self.parts.at[1 - core], self.from_core, self.sum_sem.at[0], self.sum_sem.at[1],
                sibling,
            )

        def spread(self):
            self.swapped.wait_recv()
            for k in range(CHIPS):
                band = slice(16 * k, 16 * (k + 1))
                self.mine[k] = self.parts[core, band] + self.from_core[band]
            self.copies = [
                push(
                    self.mine.at[on(o)], self.from_chips.at[o - 1], self.chip_sem.at[0, o - 1],
                    self.chip_sem.at[1, o - 1], chip_at(o),
                )
                for o in range(1, CHIPS)
            ]

        def cross(self):
            self.total = self.mine[chip]
            for o in range(1, CHIPS):
                self.copies[o - 1].wait_recv()
                self.total = self.total + self.from_chips[o - 1]
            self.leaf_sum[...] = self.total
            self.copies = [
                push(
                    self.leaf_sum, self.from_leaves.at[b - 1], self.leaf_sem.at[0, b - 1],
                    self.leaf_sem.at[1, b - 1], leaf_at(b),
                )
                for b in (1, 2, 3)
            ]

        def finish(self):
            self.copies[0].wait_recv()
            near = self.leaf_sum[...] + self.from_leaves[0]
            self.copies[1].wait_recv()
            self.copies[2].wait_recv()
            return near, self.from_leaves[1] + self.from_leaves[2]

    def gram_rings(ref, sems):
        return [
            Ring(
                lambda zz, cc, k=k: ref.at[k, zz, cc], ref.at[k, chip, core], (4 - k, 3 + k),
                sems[0].at[k], sems[1].at[k], sems[2].at[k], sems[3].at[k],
            )
            for k in (0, 1)
        ]

    pair_total, quad_total = Total(pair_parts, pair_bufs), Total(quad_parts, quad_bufs)
    pair_rings, quad_rings = gram_rings(grams_ref, gram_sems), gram_rings(quad_ref, last_sems)
    residual_b = residual8.astype(BF16)
    inner = ((0,), (0,))
    line = lax.broadcasted_iota(jnp.int32, (8, HALF), 0)

    def lines_of(k):
        rhs = dot(residual_b, upper[:, RANK * k : RANK * (k + 1)])
        rhs = rhs + dot(residual_b, lower[:, RANK * k : RANK * (k + 1)])
        return jnp.where(line == 0, rhs[:, 0:HALF], jnp.where(line == 1, rhs[:, HALF:], 0.0))

    def residue(offset, fresh=False):
        at = on(offset)
        block = cov[:, pl.ds(pl.multiple_of(at * 2 * rows, 128), 2 * rows)]
        term = dot(all_res[at].astype(BF16), block, ((1,), (1,)))
        residue_ref[...] = term if fresh else residue_ref[...] + term

    res_ring = Ring(
        lambda zz, cc: all_res.at[zz], all_res.at[chip], (4, 3), res_send, res_recv, None, None
    )
    for step in range(1, 5):
        serve(panel_rings[0], step)
        serve(panel_rings[1], step)
        if step == 1:
            res_copy.wait_recv()
            all_res[chip] = own_res[0] + own_res[1]
            res_ring.start()
        else:
            serve([res_ring], step - 1)
        absorb(0, step - 1)
        absorb(1, step - 1)
        residue(1 - step, step == 1)
        if step > 1:
            residue(step - 1)
    absorb(0, 4)
    absorb(1, 4)

    own_one = panels[0, chip, own_rows]
    own_two = panels[1, chip, own_rows]
    upper, lower = split(solved_ref[...])
    gram = dot(own_one, jnp.concatenate([upper, lower], axis=1), inner)
    gram = gram[:, 0:512] + gram[:, 512:1024]
    pair_parts[0] = gram[0:128]
    pair_parts[1, :, 0:384] = gram[128:256, 128:512]
    pair_parts[1, :, 384:512] = jnp.zeros((HALF, HALF), F32)
    pair_parts[1, 0:8, 384:512] = lines_of(0)
    pair_total.swap()
    gram = dot(own_two, jnp.concatenate([upper[:, 256:512], lower[:, 256:512]], axis=1), inner)
    gram = gram[:, 0:256] + gram[:, 256:512]
    quad_parts[0, :, 0:128] = gram[0:128, 128:256]
    quad_parts[0, :, 128:256] = jnp.zeros((HALF, HALF), F32)
    quad_parts[0, 0:8, 128:256] = lines_of(1)
    quad_parts[1, :, 0:128] = gram[0:128, 0:128]
    quad_parts[1, :, 128:256] = gram[128:256, 128:256]
    quad_total.swap()
    pair_total.spread()
    serve([res_ring], 4)
    residue(4)
    pair_total.cross()
    quad_total.spread()
    grams_ref[0, chip, core], grams_ref[1, chip, core] = pair_total.finish()
    for ring in pair_rings:
        ring.start()
    quad_total.cross()
    serve(pair_rings, 1)
    near, far = quad_total.finish()
    total = near + far
    quad_ref[0, chip, core] = total[:, 0:128]
    quad_ref[1, chip, core] = total[:, 128:256]
    for ring in quad_rings:
        ring.start()
    serve(pair_rings, 2)
    serve(quad_rings, 1)
    serve(pair_rings, 3)
    serve(quad_rings, 2)
    serve(pair_rings, 4)
    for step in range(0, 5):
        handed(pair_rings, step)

    def last_handed():
        for step in range(0, 5):
            handed(quad_rings, step)

    hooks = (lambda: serve(quad_rings, 3), lambda: serve(quad_rings, 4), last_handed)
    solve(grams_ref, quad_ref, solved_ref, residue_ref, alpha_ref, hooks)
    for copy in sent:
        copy.wait_send()


def inverse_of(value):
    guess = pl.reciprocal(value, approx=True)
    guess = guess * (2.0 - value * guess)
    return guess * (2.0 - value * guess)


def root_inverse(value):
    guess = lax.rsqrt(value)
    return guess * (1.5 - 0.5 * value * guess * guess)


def factor(matrices):
    count = len(matrices)
    tile = (8, HALF)
    left = jnp.stack(matrices).reshape(count, 16, 8, HALF)
    lane = lax.broadcasted_iota(jnp.int32, tile, 1)
    line = lax.broadcasted_iota(jnp.int32, tile, 0)

    def join(pieces):
        wide = [jnp.broadcast_to(piece, tile) for piece in pieces]
        return wide[0] if count == 1 else jnp.where(line < 4, wide[0], wide[1])

    def part(value):
        if count == 1:
            return value[None]
        return jnp.stack([jnp.broadcast_to(value[4 * k : 4 * k + 1], tile) for k in (0, 1)])

    done = []
    for group in range(16):
        start = 8 * group
        top, left = left[:, 0], left[:, 1:]
        inside = (lane >= start) & (lane < start + 8)
        rows = [join([top[k, j : j + 1] for k in range(count)]) for j in range(8)]
        p = {
            (i, j): jnp.broadcast_to(rows[i][:, start + j : start + j + 1], tile)
            for i in range(8)
            for j in range(i, 8)
        }
        rows = [
            jnp.where(inside, jnp.where(lane == start + j, 1.0, 0.0), rows[j]) for j in range(8)
        ]
        ties, scaled, final = [], [None] * 8, [None] * 8
        for i in range(0, 8, 2):
            a, b, d = p[i, i], p[i, i + 1], p[i + 1, i + 1]
            scale = inverse_of(a * d - b * b)
            i00, i01, i11 = d * scale, -b * scale, a * scale
            tie = {}
            for j in range(i + 2, 8):
                tie[j] = (
                    i00 * p[i, j] + i01 * p[i + 1, j],
                    i01 * p[i, j] + i11 * p[i + 1, j],
                )
            for m in range(i + 2, 8):
                for j in range(m, 8):
                    p[m, j] = p[m, j] - (p[i, m] * tie[j][0] + p[i + 1, m] * tie[j][1])
            for j in range(i + 2, 8):
                rows[j] = rows[j] - (tie[j][0] * rows[i] + tie[j][1] * rows[i + 1])
            scaled[i] = i00 * rows[i] + i01 * rows[i + 1]
            scaled[i + 1] = i01 * rows[i] + i11 * rows[i + 1]
            ties.append(tie)
            unit = root_inverse(a)
            final[i] = rows[i] * unit
            b = b * unit
            final[i + 1] = (rows[i + 1] - b * final[i]) * root_inverse(d - b * b)
        for i in (4, 2, 0):
            for j in range(7, i + 1, -1):
                scaled[i] = scaled[i] - ties[i // 2][j][0] * scaled[j]
                scaled[i + 1] = scaled[i + 1] - ties[i // 2][j][1] * scaled[j]
        whole = part(final[0])
        for j in range(1, 8):
            whole = jnp.where(line == j, part(final[j]), whole)
        scaled = [part(value)[:, None] for value in scaled]
        done.append(jnp.where(lane < start + 8, whole, 0.0))
        if group < 15:
            shape = left.shape
            columns = [
                jnp.broadcast_to(left[:, :, :, start + j : start + j + 1], shape)
                for j in range(8)
            ]
            left = jnp.where(inside, 0.0, left)
            for j in (6, 4, 2, 0):
                left = left - (
                    columns[j] * scaled[j] + columns[j + 1] * scaled[j + 1]
                )
    whole = jnp.stack(done, axis=1).reshape(count, HALF, HALF)
    return [whole[k] for k in range(count)]


def symmetric(block):
    return 0.5 * (block + block.T)


def solve(grams_ref, quad_ref, solved_ref, residue_ref, alpha_ref, hooks):
    line = lax.broadcasted_iota(jnp.int32, (HALF, HALF), 0)
    lane = lax.broadcasted_iota(jnp.int32, (HALF, HALF), 1)
    eye = jnp.where(line == lane, jnp.float32(1.0), 0.0)
    inner, outer = ((0,), (0,)), ((1,), (1,))

    def block(k, core, start, stop):
        return grams_ref[k, :, core, :, start:stop].reshape(HALF, stop - start)

    def quad_block(k, core):
        return quad_ref[k, :, core].reshape(HALF, HALF)

    def halves(packed):
        return [jnp.broadcast_to(packed[k : k + 1], (8, HALF)) for k in (0, 1)]

    rhs = [grams_ref[k, 0, 1, 0:8, 384:512] for k in (0, 1)]
    head = factor([eye + symmetric(block(k, 0, 0, 128)) for k in (0, 1)])
    hooks[0]()
    tie = [mid(head[k], block(k, 0, 128, 256)) for k in (0, 1)]
    rest = [eye + symmetric(block(k, 1, 0, 128)) - mid(tie[k], tie[k], inner) for k in (0, 1)]
    hooks[1]()
    tail = factor(rest)

    cross, answers = [], []
    for k in (0, 1):
        upper = mid(head[k], block(k, 0, 256, 512))
        lower = mid(tail[k], block(k, 1, 128, 384) - mid(tie[k], upper, inner))
        cross += [upper, lower]
        f0, f1 = halves(rhs[k])
        y0 = mid(f0, head[k], outer)
        answers += [y0, mid(f1 - mid(y0, tie[k]), tail[k], outer)]
    near_cross = jnp.concatenate(cross[0:2], axis=0)
    near_answers = jnp.concatenate(answers[0:2], axis=1)
    cross = jnp.concatenate(cross, axis=0)
    answers = jnp.concatenate(answers, axis=1)
    gram = mid(cross, cross, inner)
    hooks[2]()
    rest = jnp.concatenate(halves(quad_ref[1, 0, 0, 0:8]), axis=1) - mid(answers, cross)

    (quad_head,) = factor([eye + symmetric(quad_block(0, 1)) - gram[0:128, 0:128]])
    quad_tie = mid(quad_head, quad_block(0, 0) - gram[0:128, 128:256])
    (quad_tail,) = factor(
        [
            eye + symmetric(quad_block(1, 1)) - gram[128:256, 128:256]
            - mid(quad_tie, quad_tie, inner)
        ]
    )
    y0 = mid(rest[:, 0:128], quad_head, outer)
    y1 = mid(rest[:, 128:256] - mid(y0, quad_tie), quad_tail, outer)

    def back(y0, y1, first, between, last):
        x1 = mid(y1, last)
        return [mid(y0 - mid(x1, between, outer), first), x1]

    gain = back(y0, y1, quad_head, quad_tie, quad_tail)
    y = near_answers - mid(jnp.concatenate(gain, axis=1), near_cross, outer)
    shift = back(y[:, 0:128], y[:, 128:256], head[0], tie[0], tail[0])
    both = jnp.concatenate(shift + gain, axis=1)
    alpha = residue_ref[...] - mid(both, solved_ref[...], outer)
    alpha_ref[...] = alpha[0]


def per_device(inverse_cov, panel_one, panel_two, response, inputs, coeffs, degrees):
    codes, picks = degree_tables()
    rows = panel_one.shape[0]
    vmem = pl.BlockSpec(memory_space=pltpu.VMEM)
    hbm = pl.BlockSpec(memory_space=pltpu.HBM)
    dma = pltpu.SemaphoreType.DMA

    def sum_buffers(wide):
        return (
            pltpu.VMEM((HALF, wide), F32),
            pltpu.VMEM((CHIPS, 16, wide), F32),
            pltpu.VMEM((CHIPS - 1, 16, wide), F32),
            pltpu.VMEM((16, wide), F32),
            pltpu.VMEM((3, 16, wide), F32),
            dma((2,)), dma((2, CHIPS - 1)), dma((2, 3)),
        )

    ring_sems = (dma((2, 2, 4)), dma((2, 2, 4)), dma((2, 9)), dma((2, 9)))
    return pl.pallas_call(
        gather_kernel,
        out_shape=jax.ShapeDtypeStruct((rows,), F32),
        in_specs=[hbm] * 9,
        out_specs=vmem,
        scratch_shapes=[
            pltpu.VMEM((2, CHIPS, 2, 16, 512), F32),
            pltpu.VMEM((2, CHIPS, 2, 16, 128), F32),
            pltpu.VMEM((rows, 2 * RANK), F32),
            pltpu.VMEM((8, rows), F32),
            pltpu.VMEM(response.shape, F32),
            pltpu.VMEM(inputs.shape, F32),
            pltpu.VMEM(coeffs.shape, F32),
            pltpu.VMEM(degrees.shape, jnp.int32),
            pltpu.VMEM(codes.shape, jnp.int32),
            pltpu.VMEM(picks.shape, BF16),
            pltpu.VMEM(inverse_cov.shape, BF16),
            pltpu.VMEM((2, CHIPS, 2 * rows, RANK), BF16),
            pltpu.VMEM((8, rows), F32),
            pltpu.VMEM((2, 8, 2 * rows), F32),
            pltpu.VMEM((CHIPS, 8, 2 * rows), F32),
            pltpu.VMEM((2, HALF, 512), F32),
            pltpu.VMEM((2, HALF, 256), F32),
            dma((9,)),
            dma((4, 2, 4)), dma((4, 2, 4)),
            dma((4, 9)), dma((4, 9)),
            dma((2, 4)), dma((2, 4)),
            dma, dma,
            sum_buffers(512), sum_buffers(256),
            ring_sems, ring_sems,
        ],
        compiler_params=pltpu.CompilerParams(
            collective_id=0, has_side_effects=True, vmem_limit_bytes=63 * 1024 * 1024
        ),
    )(
        inverse_cov, panel_one, panel_two, response, inputs, coeffs, degrees,
        jnp.asarray(codes), jnp.asarray(picks),
    )


def solution(mesh):
    in_specs = (
        P(("runs", "rank"), None),
        P(("runs", "rank"), None),
        P(("runs", "rank"), None),
        P(("runs", "rank")),
        P(None, ("runs", "rank")),
        P(),
        P(),
    )
    out_specs = P(("runs", "rank"))
    return jax.shard_map(
        per_device, mesh=mesh, in_specs=in_specs, out_specs=out_specs, check_vma=False
    )
```
